256 devices in a mesh: dp: 64 (over z, x_lo, y), block: 4 (over x_hi, core).
Axes of the slice: x: 4 (x_hi: 2, x_lo: 2; x = x_hi * 2 + x_lo), y: 4, z: 8, core: 2. Of those that a mesh axis runs over, the one named last changes fastest.
Arguments:
- acts: bfloat16 [49152, 4096], P('dp', 'block'), as said below
- grads_out: bfloat16 [49152, 4096], P('dp', 'block'), as said below
- gradient: float32 [4, 1024, 4096], P('block', 'dp'), may hold values from -96 to 96
Outputs:
- precond: bfloat16 [4, 1024, 4096], P('block', 'dp')
The draws below stay inside these ranges and needn't reach their ends.
Inputs may be any that keep to these rules, and one draw needn't show every extreme that they name: `acts`: activations of order one with feature scales spread over a factor of about ten. `grads_out`: output gradients of order one with feature scales spread over a factor of about ten.
All inputs are finite; a program needn't handle non-finite values.
Results may differ from the reference program's by a relative error of at most 0.0022.
The reference program's roundings to bfloat16 on the way count: a program that leaves them out, or rounds other values in their place, can miss the bound.
Values may be sent and summed in bfloat16 or wider, within the bound.
No kernel may reach another device: no remote copies, remote signals or barrier semaphores. Data moves between devices by JAX's collectives and lax.ppermute only.
A program may use at most 128 MiB of HBM per device.

```python
import math
import jax
import jax.numpy as jnp
from jax import lax

BLK = 1024
ITERS = 3
DIN = 4096
DOUT = 4096
TOKENS = 49152


def shaping(key, entries, coupling):
    key_mix, key_col = jax.random.split(key, 2)
    total_rows = entries.shape[0]
    width = entries.shape[1]
    groups = width // BLK
    mixing = jax.random.normal(key_mix, (groups, BLK, BLK), jnp.float32) * (coupling / math.sqrt(BLK))
    mixing = mixing + jnp.eye(BLK, dtype=jnp.float32)[None, :, :]
    mixed = jnp.einsum('tgk,gkc->tgc', entries.reshape(total_rows, groups, BLK), mixing, precision=lax.Precision.HIGHEST)
    mixed = mixed.reshape(total_rows, width)
    col_scale = jnp.exp(jax.random.uniform(key_col, (1, width), jnp.float32, -1.2, 1.2))
    return (mixed * col_scale).astype(jnp.bfloat16)


def draw_acts(key, part):
    key = jax.random.fold_in(key, 11)
    key_base, key_shape = jax.random.split(key)
    entries = jax.random.normal(key_base, (TOKENS, DIN), jnp.float32)
    return shaping(key_shape, entries, 0.7)


def draw_grads_out(key, part):
    key = jax.random.fold_in(key, 23)
    key_base, key_shape = jax.random.split(key)
    entries = jax.random.normal(key_base, (TOKENS, DOUT), jnp.float32)
    return shaping(key_shape, entries, 0.7)


def steps_of(stream_key, extent, cuts, low, high):
    level, own = 1.0, jax.random.fold_in(stream_key, 6)
    for position, blocks in cuts:
        draws = jnp.exp(jax.random.uniform(jax.random.fold_in(own, position), (blocks,), jnp.float32, low / len(cuts), high / len(cuts)))
        level = level * jnp.repeat(draws, extent[position] // blocks).reshape([-1 if axis == position else 1 for axis in range(len(extent))])
    return level


def gaussian(stream_key, dims, scale, limit, cuts=(), held_as=jnp.bfloat16):
    array = scale * jax.random.normal(stream_key, dims, jnp.float32)
    if cuts:
        array = array * steps_of(stream_key, dims, cuts, -0.22, 0.18)
    return jnp.clip(array, -limit, limit).astype(held_as)


def setup_inputs(seed: int = 0) -> dict:
    splits = jax.random.split(jax.random.key(seed), 4)
    return {
        "acts": draw_acts(jax.random.fold_in(splits[3], 71), 0),
        "grads_out": draw_grads_out(jax.random.fold_in(splits[3], 71), 0),
        "gradient": gaussian(splits[2], (DIN // BLK, BLK, DOUT), 16.0, 96.0, ((0, 4), (1, 64)), jnp.float32),
    }


damping = 0.05

def inverse_root(columns):
    factor = jnp.dot(columns.T, columns, preferred_element_type=jnp.float32) / TOKENS
    identity = jnp.eye(BLK, dtype=jnp.float32)
    damped = factor + damping * identity
    frob_norm = jnp.sqrt(jnp.sum(damped * damped))
    scaled = (damped / frob_norm).astype(jnp.bfloat16)
    iterate = 1.5 * identity - 0.5 * scaled.astype(jnp.float32)
    for sweep in range(ITERS - 1):
        iterate_b = iterate.astype(jnp.bfloat16)
        square_b = jnp.dot(iterate_b, iterate_b, preferred_element_type=jnp.float32).astype(jnp.bfloat16)
        cubic_b = jnp.dot(square_b, scaled, preferred_element_type=jnp.float32).astype(jnp.bfloat16)
        iterate = 1.5 * iterate - 0.5 * jnp.dot(cubic_b, iterate_b, preferred_element_type=jnp.float32)
    return (iterate / jnp.sqrt(frob_norm)).astype(jnp.bfloat16)

def reference(acts, grads_out, gradient):
    count_in = DIN // BLK
    count_out = DOUT // BLK
    act_roots = [inverse_root(acts[:, number * BLK:(number + 1) * BLK]) for number in range(count_in)]
    out_roots = jnp.stack([inverse_root(grads_out[:, number * BLK:(number + 1) * BLK]) for number in range(count_out)])
    out_roots_f = out_roots.astype(jnp.float32)
    grad_b = gradient.astype(jnp.bfloat16)
    finished = []
    for number in range(count_in):
        split_cols = grad_b[number].astype(jnp.float32).reshape(BLK, count_out, BLK)
        right_done = jnp.einsum('rkc,kcd->rkd', split_cols, out_roots_f, precision=lax.Precision.HIGHEST)
        right_done = right_done.astype(jnp.bfloat16).reshape(BLK, DOUT)
        finished.append(jnp.dot(act_roots[number], right_done, preferred_element_type=jnp.float32).astype(jnp.bfloat16))
    return jnp.stack(finished)
```

```python
import jax
import jax.numpy as jnp
import numpy as np
from jax import lax
from jax.sharding import Mesh, PartitionSpec as P

ITERS = 3
DAMPING = 0.05
TILE = 128

AXES = ("z", "xl", "y", "xh", "c")
SIZES = (8, 2, 4, 2, 2)
NZ, NXL, NY, NXH, NC = SIZES

ORDER = 1024
GRID = ORDER // TILE
PAIRS = [(r, c) for r in range(GRID) for c in range(r, GRID)]
PER_Y = len(PAIRS) // NY
PIECE = PER_Y * TILE


def pack_upper(term):
    blocks = [term[r * TILE:(r + 1) * TILE, c * TILE:(c + 1) * TILE] for r, c in PAIRS]
    return jnp.concatenate(blocks, axis=0).astype(jnp.bfloat16)


def unpack_upper(packed):
    where = {pair: n for n, pair in enumerate(PAIRS)}
    rows = []
    for r in range(GRID):
        row = []
        for c in range(GRID):
            n = where[(min(r, c), max(r, c))]
            block = packed[n * TILE:(n + 1) * TILE]
            row.append(block if r <= c else block.T)
        rows.append(jnp.concatenate(row, axis=1))
    return jnp.concatenate(rows, axis=0)


def gram(columns):
    return lax.dot_general(
        columns, columns, (((0,), (0,)), ((), ())), preferred_element_type=jnp.float32
    )


def local(acts, grads_out, gradient):
    all_tokens = acts.shape[0] * NZ * NXL * NY
    y = lax.axis_index("y")
    z = lax.axis_index("z")

    grad_b = gradient[0].astype(jnp.bfloat16)
    rows = grad_b.shape[0]
    by_block = grad_b.reshape(rows, NY, ORDER).transpose(1, 0, 2)
    slab = lax.all_to_all(by_block, "y", 0, 0, tiled=True).reshape(1, NY * rows, ORDER)
    half = lax.all_to_all(
        jnp.broadcast_to(slab, (NZ, NY * rows, ORDER)), "z", 0, 0, tiled=True
    )
    other = lax.ppermute(half, "xl", [(1, 0)])
    grad_block = jnp.stack((half, other), axis=1).reshape(ORDER, ORDER)

    packed = jnp.concatenate((pack_upper(gram(acts)), pack_upper(gram(grads_out))), axis=0)
    packed = packed.reshape(NXL * NY, PIECE, TILE)
    got = lax.all_to_all(packed, ("xl", "y"), 0, 0, tiled=True)
    piece = jnp.sum(got.astype(jnp.float32), axis=0)
    got = lax.all_to_all(piece.reshape(NZ, PIECE // NZ, TILE), "z", 0, 0, tiled=True)
    part = jnp.sum(got, axis=0)
    piece = lax.all_to_all(
        jnp.broadcast_to(part[None], (NZ,) + part.shape), "z", 0, 0, tiled=True
    ).reshape(PER_Y, TILE, TILE)

    on_diag = np.array([float(r == c) for r, c in PAIRS], np.float32).reshape(NY, PER_Y)
    diag = jnp.asarray(on_diag)[y][:, None, None]
    damped = piece / all_tokens + DAMPING * diag * jnp.eye(TILE, dtype=jnp.float32)[None]
    squares = jnp.sum((2.0 - diag) * damped * damped)
    squares = jnp.full((8, TILE), squares, jnp.float32)
    total = squares
    for shift in range(1, NY):
        total = total + lax.ppermute(
            squares, "y", [(n, (n + shift) % NY) for n in range(NY)]
        )
    frob_norm = jnp.sqrt(total[0, 0])
    scaled_piece = (damped / frob_norm).astype(jnp.bfloat16).reshape(1, PIECE, TILE)
    scaled = unpack_upper(
        lax.all_to_all(
            jnp.broadcast_to(scaled_piece, (NY, PIECE, TILE)), "y", 0, 0, tiled=True
        ).reshape(NY * PIECE, TILE)
    )

    iterate = 1.5 * jnp.eye(ORDER, dtype=jnp.float32) - 0.5 * scaled.astype(jnp.float32)
    for sweep in range(ITERS - 1):
        iterate_b = iterate.astype(jnp.bfloat16)
        square_b = jnp.dot(iterate_b, iterate_b, preferred_element_type=jnp.float32).astype(jnp.bfloat16)
        cubic_b = jnp.dot(square_b, scaled, preferred_element_type=jnp.float32).astype(jnp.bfloat16)
        iterate = 1.5 * iterate - 0.5 * jnp.dot(cubic_b, iterate_b, preferred_element_type=jnp.float32)
    root = (iterate / jnp.sqrt(frob_norm)).astype(jnp.bfloat16)

    columns = lax.dynamic_slice_in_dim(root, z * TILE, TILE, axis=1)
    pairs = []
    for i in range(NXH * NC):
        for k in range(NXH * NC):
            source = (NY + i) * NXH * NC + k
            target = k * NXH * NC + i
            pairs.append((source, target))
    columns = lax.ppermute(columns, ("xl", "y", "xh", "c"), pairs)
    right_done = jnp.dot(grad_block, columns, preferred_element_type=jnp.float32).astype(jnp.bfloat16)
    result = jnp.dot(root, right_done, preferred_element_type=jnp.float32).astype(jnp.bfloat16)
    result = result.reshape(NZ * NXL * NY, rows, TILE)
    returned = lax.all_to_all(result, ("z", "xl", "y"), 0, 0, tiled=True)
    returned = returned.reshape(NZ, NXL, NY, rows, TILE)[:, 0]
    return returned.transpose(2, 1, 0, 3).reshape(1, rows, NY * NZ * TILE)


def solution(mesh):
    split = Mesh(mesh.devices.reshape(SIZES), AXES)
    dp, block = ("z", "xl", "y"), ("xh", "c")
    in_specs = (P(dp, block), P(dp, block), P(block, dp, None))
    out_specs = P(block, dp, None)
    return jax.shard_map(local, mesh=split, in_specs=in_specs, out_specs=out_specs, check_vma=False)
```

```python
import functools

import jax
import jax.numpy as jnp
import numpy as np
from jax import lax
from jax.experimental import pallas as pl
from jax.experimental.pallas import tpu as pltpu
from jax.sharding import Mesh, PartitionSpec as P

F32, BF16 = jnp.float32, jnp.bfloat16
SWEEPS = 2
DAMPING = 0.05
TILE = 128
VMEM_BYTES = 48 << 20

AXES = ("zh", "zl", "xl", "y", "xh", "c")
SIZES = (4, 2, 2, 4, 2, 2)
NZH, NZL, NXL, NY, NXH, NC = SIZES
NZ, NBLOCK = NZH * NZL, NXH * NC
DP = ("zh", "zl", "xl", "y")

ORDER = 1024
GRID = ORDER // TILE
PAIRS = [(r, c) for r in range(GRID) for c in range(r, GRID)]
WHERE = {pair: n for n, pair in enumerate(PAIRS)}
PIECE = len(PAIRS) * TILE // (NZL * NY)
SHARE = PIECE // NZH
HALF = len(PAIRS) // NZL
ON_DIAG = np.repeat(np.array([float(r == c) for r, c in PAIRS], np.float32), TILE)
ROWS = 16


def call(kernel, name, out_shape, args, specs=None, scratch=(), flops=0):
    extra = {} if specs is None else {"in_specs": specs}
    return pl.pallas_call(
        kernel,
        out_shape=out_shape,
        scratch_shapes=list(scratch),
        compiler_params=pltpu.CompilerParams(vmem_limit_bytes=VMEM_BYTES),
        cost_estimate=pl.CostEstimate(flops=flops, bytes_accessed=4 << 20, transcendentals=0),
        name=name,
        **extra,
    )(*args)


SMEM = pl.BlockSpec(memory_space=pltpu.SMEM)
VMEM = pl.BlockSpec(memory_space=pltpu.VMEM)


def gram_kernel(y_ref, acts_ref, grads_ref, gradient_ref, out_ref, *turn_refs):
    y = y_ref[0]
    for shift, ref in enumerate(turn_refs):
        start = pl.multiple_of(lax.rem(y + shift, NY) * ORDER, ORDER)
        ref[...] = gradient_ref[0, :, pl.ds(start, ORDER)].astype(BF16)
    width = 2 * TILE
    for which, ref in enumerate((acts_ref, grads_ref)):
        for first in range(0, ORDER, width):
            slab = lax.dot_general(
                ref[:, first:first + width],
                ref[:, first:],
                (((0,), (0,)), ((), ())),
                preferred_element_type=F32,
            )
            for r in range(first // TILE, (first + width) // TILE):
                for c in range(r, GRID):
                    n = WHERE[(r, c)]
                    n = ((n // HALF) * NXL + which) * HALF + n % HALF
                    out_ref[n * TILE:(n + 1) * TILE, :] = slab[
                        r * TILE - first:(r + 1) * TILE - first,
                        c * TILE - first:(c + 1) * TILE - first,
                    ].astype(BF16)


def root_kernel(z_ref, packed_ref, frob_ref, root_ref, cols_ref, scaled, iterate, iterate_b, square_b, cubic_b):
    for (r, c), n in WHERE.items():
        block = packed_ref[n * TILE:(n + 1) * TILE, :]
        scaled[r * TILE:(r + 1) * TILE, c * TILE:(c + 1) * TILE] = block
        if r != c:
            scaled[c * TILE:(c + 1) * TILE, r * TILE:(r + 1) * TILE] = block.T
    width = 2 * TILE
    tiles = [slice(n, n + width) for n in range(0, ORDER, width)]
    for s in tiles:
        row = lax.broadcasted_iota(jnp.int32, (ORDER, width), 0)
        col = lax.broadcasted_iota(jnp.int32, (ORDER, width), 1) + s.start
        first = 1.5 * (row == col).astype(F32) - 0.5 * scaled[:, s].astype(F32)
        iterate[:, s] = first
        iterate_b[:, s] = first.astype(BF16)
    root_frob = jnp.sqrt(frob_ref[0:1, 0:1])
    for sweep in range(SWEEPS):
        for s in tiles:
            square_b[:, s] = jnp.dot(
                iterate_b[...], iterate_b[:, s], preferred_element_type=F32
            ).astype(BF16)
        for s in tiles:
            cubic_b[:, s] = jnp.dot(
                square_b[...], scaled[:, s], preferred_element_type=F32
            ).astype(BF16)
        for s in tiles:
            new = 1.5 * iterate[:, s] - 0.5 * jnp.dot(
                cubic_b[...], iterate_b[:, s], preferred_element_type=F32
            )
            if sweep < SWEEPS - 1:
                iterate[:, s] = new
            else:
                root_ref[:, s] = (new / root_frob).astype(BF16)
        if sweep < SWEEPS - 1:
            for s in tiles:
                iterate_b[:, s] = iterate[:, s].astype(BF16)
    cols_ref[...] = root_ref[:, pl.ds(pl.multiple_of(z_ref[0] * TILE, TILE), TILE)]


def finish_kernel(zy_ref, cols_ref, root_ref, *refs):
    slabs, out_ref, right = refs[:2 * NZ], refs[2 * NZ], refs[2 * NZ + 1]
    z, y = zy_ref[0], zy_ref[1]
    for back in range(NZ):
        first = lax.rem(z + NZ - back, NZ) * (NXL * NY * ROWS)
        for half in range(NXL):
            done = jnp.dot(
                slabs[half * NZ + back][...], cols_ref[...], preferred_element_type=F32
            ).astype(BF16)
            for turn in range(NY):
                at = first + half * (NY * ROWS) + lax.rem(y + NY - turn, NY) * ROWS
                right[pl.ds(pl.multiple_of(at, ROWS), ROWS), :] = done[turn * ROWS:(turn + 1) * ROWS]
    out_ref[...] = jnp.dot(root_ref[...], right[...], preferred_element_type=F32).astype(BF16)


def turned(x, axes, size, shift):
    return lax.ppermute(x, axes, [(n, (n + shift) % size) for n in range(size)])


def local(acts, grads_out, gradient):
    all_tokens = acts.shape[0] * NZ * NXL * NY
    y = lax.axis_index("y")
    z = lax.axis_index(("zh", "zl"))
    piece_id = lax.axis_index(("zl", "y"))
    part_id = piece_id * NZH + lax.axis_index("zh")

    packed, *turns = call(
        gram_kernel,
        "gram",
        [jax.ShapeDtypeStruct((NXL * len(PAIRS) * TILE, TILE), BF16)]
        + [jax.ShapeDtypeStruct((ROWS, ORDER), BF16)] * NY,
        (y[None], acts, grads_out, gradient),
        specs=[SMEM, VMEM, VMEM, VMEM],
        flops=4 * acts.shape[0] * ORDER * ORDER,
    )

    slab = jnp.concatenate(
        [turns[0]] + [turned(turns[shift], "y", NY, shift) for shift in range(1, NY)], axis=0
    )
    slabs = [slab] + [turned(slab, ("zh", "zl"), NZ, shift) for shift in range(1, NZ)]
    slabs = slabs + [lax.ppermute(slab, "xl", [(1, 0)]) for slab in slabs]

    got = lax.all_to_all(
        packed.reshape(NZL * NXL * NY, PIECE, TILE), ("zl", "xl", "y"), 0, 0, tiled=True
    )
    piece = jnp.sum(got.astype(F32), axis=0)
    got = lax.all_to_all(piece.reshape(NZH, SHARE, TILE), "zh", 0, 0, tiled=True)
    part = jnp.sum(got, axis=0)

    diag = jnp.asarray(ON_DIAG.reshape(-1, SHARE, 1))[part_id]
    inner = lax.rem(part_id * SHARE + lax.broadcasted_iota(jnp.int32, (SHARE, TILE), 0), TILE)
    eye = (inner == lax.broadcasted_iota(jnp.int32, (SHARE, TILE), 1)).astype(F32)
    damped = part / all_tokens + DAMPING * diag * eye
    squares = jnp.full((8, TILE), jnp.sum((2.0 - diag) * damped * damped), F32)
    piece = lax.all_to_all(
        jnp.broadcast_to(damped[None], (NZH, SHARE, TILE)), "zh", 0, 0, tiled=True
    ).reshape(PIECE, TILE)
    squares = sum([turned(squares, ("zl", "y"), NZL * NY, s) for s in range(1, NZL * NY)], squares)
    squares = sum([turned(squares, "zh", NZH, s) for s in range(1, NZH)], squares)
    frob_norm = jnp.sqrt(squares)
    scaled_piece = (piece / frob_norm[0, 0]).astype(BF16)
    packed = lax.all_to_all(
        jnp.broadcast_to(scaled_piece[None], (NZL * NY, PIECE, TILE)), ("zl", "y"), 0, 0, tiled=True
    ).reshape(len(PAIRS) * TILE, TILE)

    square = jax.ShapeDtypeStruct((ORDER, ORDER), BF16)
    root, columns = call(
        root_kernel,
        "root",
        [square, jax.ShapeDtypeStruct((ORDER, TILE), BF16)],
        (z[None], packed, frob_norm),
        specs=[SMEM, VMEM, VMEM],
        scratch=[
            pltpu.VMEM((ORDER, ORDER), BF16),
            pltpu.VMEM((ORDER, ORDER), F32),
            pltpu.VMEM((ORDER, ORDER), BF16),
            pltpu.VMEM((ORDER, ORDER), BF16),
            pltpu.VMEM((ORDER, ORDER), BF16),
        ],
        flops=6 * SWEEPS * ORDER**3,
    )

    pairs = [
        ((NY + i) * NBLOCK + k, k * NBLOCK + i) for i in range(NBLOCK) for k in range(NBLOCK)
    ]
    columns = lax.ppermute(columns, ("xl", "y", "xh", "c"), pairs)
    result = call(
        finish_kernel,
        "finish",
        jax.ShapeDtypeStruct((ORDER, TILE), BF16),
        (jnp.stack((z, y)), columns, root, *slabs),
        specs=[SMEM] + [VMEM] * (2 + 2 * NZ),
        scratch=[pltpu.VMEM((ORDER, TILE), BF16)],
        flops=4 * ORDER * ORDER * TILE,
    )
    result = result.reshape(NZ * NXL * NY, ROWS, TILE)
    returned = lax.all_to_all(result, DP, 0, 0, tiled=True)
    returned = returned.reshape(NZ, NXL, NY, ROWS, TILE)[:, 0]
    return returned.transpose(2, 1, 0, 3).reshape(1, ROWS, NY * NZ * TILE)


def solution(mesh):
    split = Mesh(mesh.devices.reshape(SIZES), AXES)
    block = ("xh", "c")
    in_specs = (P(DP, block), P(DP, block), P(block, DP, None))
    out_specs = P(block, DP, None)
    return jax.shard_map(local, mesh=split, in_specs=in_specs, out_specs=out_specs, check_vma=False)
```

```python
import functools

import jax
import jax.numpy as jnp
from jax import lax
from jax.experimental import pallas as pl
from jax.experimental.pallas import tpu as pltpu
from jax.sharding import Mesh, PartitionSpec as P

F32, BF16 = jnp.float32, jnp.bfloat16
SWEEPS = 2
DAMPING = 0.05
TILE = 128
VMEM_BYTES = 48 << 20

AXES = ("zh", "zl", "xl", "y", "xh", "c")
SIZES = (4, 2, 2, 4, 2, 2)
NZH, NZL, NXL, NY, NXH, NC = SIZES
NZ, NBLOCK = NZH * NZL, NXH * NC
DP = ("zh", "zl", "xl", "y")

ORDER = 1024
GRID = ORDER // TILE
PAIRS = [(r, c) for r in range(GRID) for c in range(r, GRID)]
WHERE = {pair: n for n, pair in enumerate(PAIRS)}

HALF = TILE // 2
HALVES = 2 * len(PAIRS) // (NZL * NY)
PIECE = HALVES * HALF
REST = 16
ROWS = 16
LOADS = 4


def call(kernel, name, out_shape, args, specs=None, scratch=(), flops=0, vmem=VMEM_BYTES):
    extra = {} if specs is None else {"in_specs": specs}
    return pl.pallas_call(
        kernel,
        out_shape=out_shape,
        scratch_shapes=list(scratch),
        compiler_params=pltpu.CompilerParams(vmem_limit_bytes=vmem),
        cost_estimate=pl.CostEstimate(flops=flops, bytes_accessed=4 << 20, transcendentals=0),
        name=name,
        **extra,
    )(*args)


SMEM = pl.BlockSpec(memory_space=pltpu.SMEM)
VMEM = pl.BlockSpec(memory_space=pltpu.VMEM)


def gram_kernel(y_ref, acts_ref, grads_ref, gradient_ref, out_ref, *refs):
    turn_refs, (acts, grads, gradient, sems, gradient_sem) = refs[:NY], refs[NY:]
    rows = acts.shape[0] // LOADS
    loads = []
    for which, (far, near) in enumerate(((acts_ref, acts), (grads_ref, grads))):
        for n in range(LOADS):
            part = pl.ds(n * rows, rows)
            loads.append(pltpu.make_async_copy(far.at[part], near.at[part], sems.at[which, n]))
            loads[-1].start()
    gradient_load = pltpu.make_async_copy(gradient_ref, gradient, gradient_sem)
    gradient_load.start()
    width = 2 * TILE
    eye = lax.broadcasted_iota(jnp.int32, (TILE, TILE), 0) == lax.broadcasted_iota(
        jnp.int32, (TILE, TILE), 1
    )
    for which, ref in enumerate((acts, grads)):
        for load in loads[which * LOADS:(which + 1) * LOADS]:
            load.wait()
        rest = {}
        for first in range(0, ORDER, width):
            slab = lax.dot_general(
                ref[:, first:first + width],
                ref[:, first:],
                (((0,), (0,)), ((), ())),
                preferred_element_type=F32,
            )
            for r in range(first // TILE, (first + width) // TILE):
                for c in range(r, GRID):
                    block = slab[
                        r * TILE - first:(r + 1) * TILE - first,
                        c * TILE - first:(c + 1) * TILE - first,
                    ]
                    block_b = block.astype(BF16)
                    for half in range(2):
                        piece, at = divmod(2 * WHERE[(r, c)] + half, HALVES)
                        out_ref[target_of(which, piece), at * HALF:(at + 1) * HALF] = block_b[
                            half * HALF:(half + 1) * HALF
                        ]
                        if r == c:
                            rest[(piece, at)] = jnp.sum(
                                jnp.where(eye, block - block_b.astype(F32), 0.0), axis=0, keepdims=True
                            )
        for piece in range(NZL * NY):
            lines = [rest.get((piece, at), jnp.zeros((1, TILE), F32)) for at in range(HALVES)]
            put_rest(out_ref.at[target_of(which, piece)], lines)
    gradient_load.wait()
    for shift, ref in enumerate(turn_refs):
        start = pl.multiple_of(lax.rem(y_ref[0] + shift, NY) * ORDER, ORDER)
        ref[...] = gradient[0, :, pl.ds(start, ORDER)].astype(BF16)


def target_of(which, piece):
    return (piece // NY * NXL + which) * NY + piece % NY


def put_rest(ref, lines):
    lines = lines + [jnp.zeros((1, TILE), F32)] * (REST - len(lines))
    ref[PIECE:PIECE + REST] = jnp.concatenate(lines, axis=0).astype(BF16)


def eye_of(piece, at):
    row = lax.broadcasted_iota(jnp.int32, (HALF, TILE), 0)
    return row + lax.rem(piece * HALVES + at, 2) * HALF == lax.broadcasted_iota(
        jnp.int32, (HALF, TILE), 1
    )


def sum_halves(piece, got_ref):
    count = got_ref.shape[0]
    rest = sum([got_ref[n, PIECE:].astype(F32) for n in range(1, count)], got_ref[0, PIECE:].astype(F32))
    halves = []
    for at in range(HALVES):
        s = slice(at * HALF, (at + 1) * HALF)
        total = sum([got_ref[n, s].astype(F32) for n in range(1, count)], got_ref[0, s].astype(F32))
        halves.append(total + jnp.where(eye_of(piece, at), rest[at:at + 1], 0.0))
    return halves


def put_halves(piece, out_ref, halves):
    lines = []
    for at, half in enumerate(halves):
        half_b = half.astype(BF16)
        lines.append(
            jnp.sum(jnp.where(eye_of(piece, at), half - half_b.astype(F32), 0.0), axis=0, keepdims=True)
        )
        for n in range(out_ref.shape[0]):
            out_ref[n, at * HALF:(at + 1) * HALF] = half_b
    for n in range(out_ref.shape[0]):
        put_rest(out_ref.at[n], lines)


def sum_kernel(where_ref, got_ref, *refs):
    turn_refs, (out_ref, slab_ref) = refs[:NY], refs[NY:]
    for turn, ref in enumerate(turn_refs):
        at = lax.rem(where_ref[1] + NY - turn, NY) * ROWS
        slab_ref[pl.ds(pl.multiple_of(at, ROWS), ROWS), :] = ref[...]
    put_halves(where_ref[0], out_ref, sum_halves(where_ref[0], got_ref))


def damp_kernel(all_tokens, where_ref, got_ref, slab0_ref, slab1_ref, out_ref):
    piece = where_ref[0]
    halves = []
    for at, half in enumerate(sum_halves(piece, got_ref)):
        block = lax.div(piece * HALVES + at, 2)
        on_diag = functools.reduce(jnp.logical_or, [block == WHERE[(r, r)] for r in range(GRID)])
        damping = jnp.where(on_diag, DAMPING, 0.0)
        halves.append(half / all_tokens + jnp.where(eye_of(piece, at), damping, 0.0))
    put_halves(piece, out_ref, halves)


def root_kernel(packed_ref, slab0_ref, slab1_ref, root_ref, right_ref,
                scaled, iterate, iterate_b, square_b, cubic_b):
    def block_of(r, c):
        parts = []
        for half in range(2):
            piece, at = divmod(2 * WHERE[(r, c)] + half, HALVES)
            part = packed_ref[piece, at * HALF:(at + 1) * HALF].astype(F32)
            if r == c:
                rest = packed_ref[piece, PIECE:].astype(F32)[at:at + 1]
                part = part + jnp.where(eye_of(piece, at), rest, 0.0)
            parts.append(part)
        return jnp.concatenate(parts, axis=0)

    squares = {True: jnp.zeros((TILE, TILE), F32), False: jnp.zeros((TILE, TILE), F32)}
    for r, c in PAIRS:
        block = block_of(r, c)
        squares[r == c] = squares[r == c] + block * block
    total = jnp.sum(squares[True] + 2.0 * squares[False], axis=1, keepdims=True)
    frob = jnp.sqrt(jnp.sum(total, axis=0, keepdims=True))
    for r, c in PAIRS:
        block = (block_of(r, c) / frob).astype(BF16)
        scaled[r * TILE:(r + 1) * TILE, c * TILE:(c + 1) * TILE] = block
        if r != c:
            scaled[c * TILE:(c + 1) * TILE, r * TILE:(r + 1) * TILE] = block.T
    width = 2 * TILE
    tiles = [slice(n, n + width) for n in range(0, ORDER, width)]
    for s in tiles:
        row = lax.broadcasted_iota(jnp.int32, (ORDER, width), 0)
        col = lax.broadcasted_iota(jnp.int32, (ORDER, width), 1) + s.start
        first = 1.5 * (row == col).astype(F32) - 0.5 * scaled[:, s].astype(F32)
        iterate[:, s] = first
        iterate_b[:, s] = first.astype(BF16)
    root_frob = jnp.sqrt(frob)
    for sweep in range(SWEEPS):
        for s in tiles:
            square_b[:, s] = jnp.dot(
                iterate_b[...], iterate_b[:, s], preferred_element_type=F32
            ).astype(BF16)
        for s in tiles:
            cubic_b[:, s] = jnp.dot(
                square_b[...], scaled[:, s], preferred_element_type=F32
            ).astype(BF16)
        for s in tiles:
            new = 1.5 * iterate[:, s] - 0.5 * jnp.dot(
                cubic_b[...], iterate_b[:, s], preferred_element_type=F32
            )
            if sweep < SWEEPS - 1:
                iterate[:, s] = new
            else:
                new = (new / root_frob).astype(BF16)
                root_ref[:, s] = new
                for half, ref in enumerate((slab0_ref, slab1_ref)):
                    done = jnp.dot(ref[...], new, preferred_element_type=F32).astype(BF16)
                    for n in range(width // TILE):
                        right_ref[
                            s.start // TILE + n, half * NY * ROWS:(half + 1) * NY * ROWS
                        ] = done[:, n * TILE:(n + 1) * TILE]
        if sweep < SWEEPS - 1:
            for s in tiles:
                iterate_b[:, s] = iterate[:, s].astype(BF16)


def left_kernel(root_ref, right_ref, out_ref):
    out_ref[...] = jnp.dot(root_ref[...], right_ref[...], preferred_element_type=F32).astype(BF16)


def turned(x, axes, size, shift):
    return lax.ppermute(x, axes, [(n, (n + shift) % size) for n in range(size)])


def local(acts, grads_out, gradient):
    all_tokens = acts.shape[0] * NZ * NXL * NY
    y = lax.axis_index("y")
    where = jnp.stack((lax.axis_index(("zl", "y")), y))

    packed, *turns = call(
        gram_kernel,
        "gram",
        [jax.ShapeDtypeStruct((NZL * NXL * NY, PIECE + REST, TILE), BF16)]
        + [jax.ShapeDtypeStruct((ROWS, ORDER), BF16)] * NY,
        (y[None], acts, grads_out, gradient),
        specs=[SMEM] + [pl.BlockSpec(memory_space=pltpu.HBM)] * 3,
        scratch=[
            pltpu.VMEM(acts.shape, BF16),
            pltpu.VMEM(acts.shape, BF16),
            pltpu.VMEM(gradient.shape, F32),
            pltpu.SemaphoreType.DMA((2, LOADS)),
            pltpu.SemaphoreType.DMA(()),
        ],
        flops=4 * acts.shape[0] * ORDER * ORDER,
        vmem=60 << 20,
    )
    turns = [turns[0]] + [turned(turns[shift], "y", NY, shift) for shift in range(1, NY)]

    got = lax.all_to_all(packed, ("zl", "xl", "y"), 0, 0, tiled=True)
    pieces, slab = call(
        sum_kernel,
        "sum",
        [
            jax.ShapeDtypeStruct((NZH, PIECE + REST, TILE), BF16),
            jax.ShapeDtypeStruct((NY * ROWS, ORDER), BF16),
        ],
        (where, got, *turns),
        specs=[SMEM] + [VMEM] * (1 + NY),
    )
    cells = [(k, i) for k in range(NBLOCK) for i in range(NBLOCK)]
    slabs = [
        lax.ppermute(
            slab,
            ("xl", "y", "xh", "c"),
            [((xl * NY + k) * NBLOCK + i, (NY + i) * NBLOCK + k) for k, i in cells],
        )
        for xl in range(NXL)
    ]
    got = lax.all_to_all(pieces, "zh", 0, 0, tiled=True)
    pieces = call(
        functools.partial(damp_kernel, float(all_tokens)),
        "damp",
        jax.ShapeDtypeStruct((NZL * NY, PIECE + REST, TILE), BF16),
        (where, got, *slabs),
        specs=[SMEM, VMEM, pl.BlockSpec(memory_space=pl.ANY), pl.BlockSpec(memory_space=pl.ANY)],
    )
    packed = lax.all_to_all(pieces, ("zl", "y"), 0, 0, tiled=True)

    square_b = pltpu.VMEM((ORDER, ORDER), BF16)
    root, right_done = call(
        root_kernel,
        "root",
        [
            jax.ShapeDtypeStruct((ORDER, ORDER), BF16),
            jax.ShapeDtypeStruct((NZ, NXL * NY * ROWS, TILE), BF16),
        ],
        (packed, *slabs),
        scratch=[square_b, pltpu.VMEM((ORDER, ORDER), F32), square_b, square_b, square_b],
        flops=6 * SWEEPS * ORDER**3,
    )

    right_done = lax.all_to_all(right_done, ("zh", "zl"), 0, 0, tiled=True)
    right_done = lax.ppermute(
        right_done,
        ("xl", "y", "xh", "c"),
        [((NY + i) * NBLOCK + k, k * NBLOCK + i) for k, i in cells],
    )
    result = call(
        left_kernel,
        "left",
        jax.ShapeDtypeStruct((ORDER, TILE), BF16),
        (root, right_done.reshape(ORDER, TILE)),
        flops=2 * ORDER * ORDER * TILE,
    )
    result = result.reshape(NZ * NXL * NY, ROWS, TILE)
    returned = lax.all_to_all(result, DP, 0, 0, tiled=True)
    returned = returned.reshape(NZ, NXL, NY, ROWS, TILE)[:, 0]
    return returned.transpose(2, 1, 0, 3).reshape(1, ROWS, NY * NZ * TILE)


def solution(mesh):
    split = Mesh(mesh.devices.reshape(SIZES), AXES)
    block = ("xh", "c")
    in_specs = (P(DP, block), P(DP, block), P(block, DP, None))
    out_specs = P(block, DP, None)
    return jax.shard_map(local, mesh=split, in_specs=in_specs, out_specs=out_specs, check_vma=False)
```

```python
import functools

import jax
import jax.numpy as jnp
from jax import lax
from jax.experimental import pallas as pl
from jax.experimental.pallas import tpu as pltpu
from jax.sharding import Mesh, PartitionSpec as P

F32, BF16 = jnp.float32, jnp.bfloat16
SWEEPS = 2
DAMPING = 0.05
TILE = 128
VMEM_BYTES = 48 << 20

AXES = ("zh", "zl", "xl", "y", "xh", "c")
SIZES = (4, 2, 2, 4, 2, 2)
NZH, NZL, NXL, NY, NXH, NC = SIZES
NZ, NBLOCK = NZH * NZL, NXH * NC
DP = ("zh", "zl", "xl", "y")

ORDER = 1024
GRID = ORDER // TILE
PAIRS = [(r, c) for r in range(GRID) for c in range(r, GRID)]
WHERE = {pair: n for n, pair in enumerate(PAIRS)}

HALF = TILE // 2
HALVES = 2 * len(PAIRS) // (NZL * NY)
PIECE = HALVES * HALF
REST = 16
ROWS = 16
TERMS = 3
LOADS = 4
ZROWS = NZL * NXL * NY * ROWS


def call(kernel, name, out_shape, args, specs=None, scratch=(), flops=0, vmem=VMEM_BYTES):
    extra = {} if specs is None else {"in_specs": specs}
    return pl.pallas_call(
        kernel,
        out_shape=out_shape,
        scratch_shapes=list(scratch),
        compiler_params=pltpu.CompilerParams(vmem_limit_bytes=vmem),
        cost_estimate=pl.CostEstimate(flops=flops, bytes_accessed=4 << 20, transcendentals=0),
        name=name,
        **extra,
    )(*args)


SMEM = pl.BlockSpec(memory_space=pltpu.SMEM)
VMEM = pl.BlockSpec(memory_space=pltpu.VMEM)


def gram_kernel(y_ref, acts_ref, grads_ref, gradient_ref, out_ref, *refs):
    turn_refs, (acts, grads, gradient, sems, gradient_sem) = refs[:NY], refs[NY:]
    rows = acts.shape[0] // LOADS
    loads = []
    for which, (far, near) in enumerate(((acts_ref, acts), (grads_ref, grads))):
        for n in range(LOADS):
            part = pl.ds(n * rows, rows)
            loads.append(pltpu.make_async_copy(far.at[part], near.at[part], sems.at[which, n]))
            loads[-1].start()
    gradient_load = pltpu.make_async_copy(gradient_ref, gradient, gradient_sem)
    gradient_load.start()
    width = 2 * TILE
    eye = lax.broadcasted_iota(jnp.int32, (TILE, TILE), 0) == lax.broadcasted_iota(
        jnp.int32, (TILE, TILE), 1
    )
    for which, ref in enumerate((acts, grads)):
        for load in loads[which * LOADS:(which + 1) * LOADS]:
            load.wait()
        rest = {}
        for first in range(0, ORDER, width):
            slab = lax.dot_general(
                ref[:, first:first + width],
                ref[:, first:],
                (((0,), (0,)), ((), ())),
                preferred_element_type=F32,
            )
            for r in range(first // TILE, (first + width) // TILE):
                for c in range(r, GRID):
                    block = slab[
                        r * TILE - first:(r + 1) * TILE - first,
                        c * TILE - first:(c + 1) * TILE - first,
                    ]
                    block_b = block.astype(BF16)
                    for half in range(2):
                        piece, at = divmod(2 * WHERE[(r, c)] + half, HALVES)
                        out_ref[target_of(which, piece), at * HALF:(at + 1) * HALF] = block_b[
                            half * HALF:(half + 1) * HALF
                        ]
                        if r == c:
                            rest[(piece, at)] = jnp.sum(
                                jnp.where(eye, block - block_b.astype(F32), 0.0), axis=0, keepdims=True
                            )
        for piece in range(NZL * NY):
            lines = [rest.get((piece, at), jnp.zeros((1, TILE), F32)) for at in range(HALVES)]
            put_rest(out_ref.at[target_of(which, piece)], lines)
    gradient_load.wait()
    for shift, ref in enumerate(turn_refs):
        start = pl.multiple_of(lax.rem(y_ref[0] + shift, NY) * ORDER, ORDER)
        ref[...] = gradient[0, :, pl.ds(start, ORDER)].astype(BF16)


def target_of(which, piece):
    return (piece // NY * NXL + which) * NY + piece % NY


def put_rest(ref, lines):
    lines = lines + [jnp.zeros((1, TILE), F32)] * (REST - len(lines))
    ref[PIECE:PIECE + REST] = jnp.concatenate(lines, axis=0).astype(BF16)


def eye_of(piece, at):
    row = lax.broadcasted_iota(jnp.int32, (HALF, TILE), 0)
    return row + lax.rem(piece * HALVES + at, 2) * HALF == lax.broadcasted_iota(
        jnp.int32, (HALF, TILE), 1
    )


def sum_halves(piece, got_ref):
    count = got_ref.shape[0]
    rest = sum([got_ref[n, PIECE:].astype(F32) for n in range(1, count)], got_ref[0, PIECE:].astype(F32))
    halves = []
    for at in range(HALVES):
        s = slice(at * HALF, (at + 1) * HALF)
        total = sum([got_ref[n, s].astype(F32) for n in range(1, count)], got_ref[0, s].astype(F32))
        halves.append(total + jnp.where(eye_of(piece, at), rest[at:at + 1], 0.0))
    return halves


def put_halves(piece, out_ref, halves, more=()):
    lines = []
    for at, half in enumerate(halves):
        half_b = half.astype(BF16)
        lines.append(
            jnp.sum(jnp.where(eye_of(piece, at), half - half_b.astype(F32), 0.0), axis=0, keepdims=True)
        )
        for n in range(out_ref.shape[0]):
            out_ref[n, at * HALF:(at + 1) * HALF] = half_b
    for n in range(out_ref.shape[0]):
        put_rest(out_ref.at[n], lines + list(more))


def sum_kernel(where_ref, got_ref, *refs):
    turn_refs, (out_ref, slab_ref) = refs[:NY], refs[NY:]
    for turn, ref in enumerate(turn_refs):
        at = lax.rem(where_ref[1] + NY - turn, NY) * ROWS
        slab_ref[pl.ds(pl.multiple_of(at, ROWS), ROWS), :] = ref[...]
    put_halves(where_ref[0], out_ref, sum_halves(where_ref[0], got_ref))


def damp_kernel(all_tokens, where_ref, got_ref, *refs):
    out_ref = refs[-1]
    piece = where_ref[0]
    halves = []
    squares = jnp.zeros((HALF, TILE), F32)
    for at, half in enumerate(sum_halves(piece, got_ref)):
        block = lax.div(piece * HALVES + at, 2)
        on_diag = functools.reduce(jnp.logical_or, [block == WHERE[(r, r)] for r in range(GRID)])
        damping = jnp.where(on_diag, DAMPING, 0.0)
        half = half / all_tokens + jnp.where(eye_of(piece, at), damping, 0.0)
        squares = squares + jnp.where(on_diag, 1.0, 2.0) * half * half
        halves.append(half)
    left = jnp.sum(jnp.sum(squares, axis=0, keepdims=True), axis=1, keepdims=True)
    left = jnp.broadcast_to(left, (1, TILE))
    terms = []
    for _ in range(TERMS):
        terms.append(left.astype(BF16).astype(F32))
        left = left - terms[-1]
    put_halves(piece, out_ref, halves, terms)


def root_kernel(where_ref, packed_ref, *refs):
    slab_refs, refs = refs[:NZL * NXL], refs[NZL * NXL:]
    root_ref, right_refs, refs = refs[0], refs[1:1 + NZH], refs[1 + NZH:]
    scaled, iterate, iterate_b, square_b, cubic_b, right = refs
    terms = sum([packed_ref[n, PIECE:].astype(F32) for n in range(NZL * NY)])[HALVES:HALVES + TERMS]
    frob = jnp.sqrt(jnp.sum(terms, axis=0, keepdims=True)[:, 0:1])
    over_frob = 1.0 / frob
    over_root = 1.0 / jnp.sqrt(frob)
    for r, c in PAIRS:
        parts = []
        for half in range(2):
            piece, at = divmod(2 * WHERE[(r, c)] + half, HALVES)
            part = packed_ref[piece, at * HALF:(at + 1) * HALF].astype(F32)
            if r == c:
                rest = packed_ref[piece, PIECE:].astype(F32)[at:at + 1]
                part = part + jnp.where(eye_of(piece, at), rest, 0.0)
            parts.append(part)
        block = (jnp.concatenate(parts, axis=0) * over_frob).astype(BF16)
        scaled[r * TILE:(r + 1) * TILE, c * TILE:(c + 1) * TILE] = block
        if r != c:
            scaled[c * TILE:(c + 1) * TILE, r * TILE:(r + 1) * TILE] = block.T
    width = 2 * TILE
    tiles = [slice(n, n + width) for n in range(0, ORDER, width)]
    for s in tiles:
        row = lax.broadcasted_iota(jnp.int32, (ORDER, width), 0)
        col = lax.broadcasted_iota(jnp.int32, (ORDER, width), 1) + s.start
        first = 1.5 * (row == col).astype(F32) - 0.5 * scaled[:, s].astype(F32)
        iterate[:, s] = first
        iterate_b[:, s] = first.astype(BF16)
    for sweep in range(SWEEPS):
        for s in tiles:
            square_b[:, s] = jnp.dot(
                iterate_b[...], iterate_b[:, s], preferred_element_type=F32
            ).astype(BF16)
        for s in tiles:
            cubic_b[:, s] = jnp.dot(
                square_b[...], scaled[:, s], preferred_element_type=F32
            ).astype(BF16)
        for s in tiles:
            new = 1.5 * iterate[:, s] - 0.5 * jnp.dot(
                cubic_b[...], iterate_b[:, s], preferred_element_type=F32
            )
            if sweep < SWEEPS - 1:
                iterate[:, s] = new
            else:
                root_ref[:, s] = (new * over_root).astype(BF16)
        if sweep < SWEEPS - 1:
            for s in tiles:
                iterate_b[:, s] = iterate[:, s].astype(BF16)
    zh, zl = where_ref[0], where_ref[1]
    cols = root_ref[:, pl.ds(pl.multiple_of(zl * (NZH * TILE), NZH * TILE), NZH * TILE)]
    for turn, ref in enumerate(slab_refs):
        from_zl = lax.rem(zl + turn // NXL, NZL)
        at = (from_zl * NXL + turn % NXL) * (NY * ROWS)
        right[pl.ds(pl.multiple_of(at, NY * ROWS), NY * ROWS), :] = jnp.dot(
            ref[...], cols, preferred_element_type=F32
        ).astype(BF16)
    for shift, ref in enumerate(right_refs):
        at = lax.rem(zh + shift, NZH) * TILE
        ref[...] = right[:, pl.ds(pl.multiple_of(at, TILE), TILE)]


def left_kernel(where_ref, root_ref, *refs):
    right_refs, (out_ref, right) = refs[:NZH], refs[NZH:]
    for shift, ref in enumerate(right_refs):
        at = lax.rem(where_ref[0] + NZH - shift, NZH) * ZROWS
        right[pl.ds(pl.multiple_of(at, ZROWS), ZROWS), :] = ref[...]
    out_ref[...] = jnp.dot(root_ref[...], right[...], preferred_element_type=F32).astype(BF16)


def place(zl, xl, y, block):
    return ((zl * NXL + xl) * NY + y) * NBLOCK + block


def turned(x, axes, size, shift):
    return lax.ppermute(x, axes, [(n, (n + shift) % size) for n in range(size)])


def local(acts, grads_out, gradient):
    all_tokens = acts.shape[0] * NZ * NXL * NY
    y = lax.axis_index("y")
    where = jnp.stack((lax.axis_index(("zl", "y")), y))

    packed, *turns = call(
        gram_kernel,
        "gram",
        [jax.ShapeDtypeStruct((NZL * NXL * NY, PIECE + REST, TILE), BF16)]
        + [jax.ShapeDtypeStruct((ROWS, ORDER), BF16)] * NY,
        (y[None], acts, grads_out, gradient),
        specs=[SMEM] + [pl.BlockSpec(memory_space=pltpu.HBM)] * 3,
        scratch=[
            pltpu.VMEM(acts.shape, BF16),
            pltpu.VMEM(acts.shape, BF16),
            pltpu.VMEM(gradient.shape, F32),
            pltpu.SemaphoreType.DMA((2, LOADS)),
            pltpu.SemaphoreType.DMA(()),
        ],
        flops=4 * acts.shape[0] * ORDER * ORDER,
        vmem=60 << 20,
    )
    turns = [turns[0]] + [turned(turns[shift], "y", NY, shift) for shift in range(1, NY)]

    got = lax.all_to_all(packed, ("zl", "xl", "y"), 0, 0, tiled=True)
    pieces, slab = call(
        sum_kernel,
        "sum",
        [
            jax.ShapeDtypeStruct((NZH, PIECE + REST, TILE), BF16),
            jax.ShapeDtypeStruct((NY * ROWS, ORDER), BF16),
        ],
        (where, got, *turns),
        specs=[SMEM] + [VMEM] * (1 + NY),
    )
    cells = [(k, i) for k in range(NBLOCK) for i in range(NBLOCK)]
    count = NZL * NXL * NY * NBLOCK
    slabs = [
        lax.ppermute(
            slab,
            ("zl", "xl", "y", "xh", "c"),
            [
                (place((zl + turn) % NZL, xl, k, i), place(zl, 1, i, k))
                for zl in range(NZL)
                for k, i in cells
            ],
        )
        for turn in range(NZL)
        for xl in range(NXL)
    ]
    got = lax.all_to_all(pieces, "zh", 0, 0, tiled=True)
    pieces = call(
        functools.partial(damp_kernel, float(all_tokens)),
        "damp",
        jax.ShapeDtypeStruct((NZL * NY, PIECE + REST, TILE), BF16),
        (where, got, *slabs),
        specs=[SMEM, VMEM] + [pl.BlockSpec(memory_space=pl.ANY)] * len(slabs),
    )
    packed = lax.all_to_all(pieces, ("zl", "y"), 0, 0, tiled=True)

    square_b = pltpu.VMEM((ORDER, ORDER), BF16)
    z_where = jnp.stack((lax.axis_index("zh"), lax.axis_index("zl")))
    right_done = jax.ShapeDtypeStruct((ZROWS, TILE), BF16)
    root, *right_done = call(
        root_kernel,
        "root",
        [jax.ShapeDtypeStruct((ORDER, ORDER), BF16)] + [right_done] * NZH,
        (z_where, packed, *slabs),
        specs=[SMEM] + [VMEM] * (1 + len(slabs)),
        scratch=[square_b, pltpu.VMEM((ORDER, ORDER), F32), square_b, square_b, square_b,
                 pltpu.VMEM((ZROWS, NZH * TILE), BF16)],
        flops=6 * SWEEPS * ORDER**3,
    )

    right_done = [
        lax.ppermute(
            right_done[shift],
            ("zh", "zl", "xl", "y", "xh", "c"),
            [
                (zh * count + place(zl, 1, i, k), (zh + shift) % NZH * count + place(zl, 0, k, i))
                for zh in range(NZH)
                for zl in range(NZL)
                for k, i in cells
            ],
        )
        for shift in range(NZH)
    ]
    result = call(
        left_kernel,
        "left",
        jax.ShapeDtypeStruct((ORDER, TILE), BF16),
        (z_where, root, *right_done),
        specs=[SMEM] + [VMEM] * (1 + NZH),
        scratch=[pltpu.VMEM((ORDER, TILE), BF16)],
        flops=2 * ORDER * ORDER * TILE,
    )
    result = result.reshape(NZ * NXL * NY, ROWS, TILE)
    returned = lax.all_to_all(result, DP, 0, 0, tiled=True)
    returned = returned.reshape(NZH, NZL, NXL, NY, ROWS, TILE)[:, :, 0]
    return returned.transpose(3, 2, 1, 0, 4).reshape(1, ROWS, NY * NZ * TILE)


def solution(mesh):
    split = Mesh(mesh.devices.reshape(SIZES), AXES)
    block = ("xh", "c")
    in_specs = (P(DP, block), P(DP, block), P(block, DP, None))
    out_specs = P(block, DP, None)
    return jax.shard_map(local, mesh=split, in_specs=in_specs, out_specs=out_specs, check_vma=False)
```

```python
import functools

import jax
import jax.numpy as jnp
from jax import lax
from jax.experimental import pallas as pl
from jax.experimental.pallas import tpu as pltpu
from jax.sharding import Mesh, PartitionSpec as P

F32, BF16 = jnp.float32, jnp.bfloat16
SWEEPS = 2
DAMPING = 0.05
TILE = 128
VMEM_BYTES = 48 << 20

AXES = ("zh", "zl", "xl", "y", "xh", "c")
SIZES = (4, 2, 2, 4, 2, 2)
NZH, NZL, NXL, NY, NXH, NC = SIZES
NZ, NBLOCK = NZH * NZL, NXH * NC
DP = ("zh", "zl", "xl", "y")

ORDER = 1024
GRID = ORDER // TILE
PAIRS = [(r, c) for r in range(GRID) for c in range(r, GRID)]
WHERE = {pair: n for n, pair in enumerate(PAIRS)}

HALF = TILE // 2
HALVES = 2 * len(PAIRS) // (NZL * NY)
PIECE = HALVES * HALF
REST = 16
ROWS = 16
TERMS = 3
LOADS = 4
ZROWS = NZL * NXL * NY * ROWS


def call(kernel, name, out_shape, args, specs=None, scratch=(), flops=0, vmem=VMEM_BYTES):
    extra = {} if specs is None else {"in_specs": specs}
    return pl.pallas_call(
        kernel,
        out_shape=out_shape,
        scratch_shapes=list(scratch),
        compiler_params=pltpu.CompilerParams(vmem_limit_bytes=vmem),
        cost_estimate=pl.CostEstimate(flops=flops, bytes_accessed=4 << 20, transcendentals=0),
        name=name,
        **extra,
    )(*args)


SMEM = pl.BlockSpec(memory_space=pltpu.SMEM)
VMEM = pl.BlockSpec(memory_space=pltpu.VMEM)


def gram_kernel(y_ref, acts_ref, grads_ref, gradient_ref, out_ref, *refs):
    turn_refs, (acts, grads, gradient, sems, gradient_sem) = refs[:NY], refs[NY:]
    rows = acts.shape[0] // LOADS
    loads = []
    for which, (far, near) in enumerate(((acts_ref, acts), (grads_ref, grads))):
        for n in range(LOADS):
            part = pl.ds(n * rows, rows)
            loads.append(pltpu.make_async_copy(far.at[part], near.at[part], sems.at[which, n]))
            loads[-1].start()
    gradient_load = pltpu.make_async_copy(gradient_ref, gradient, gradient_sem)
    gradient_load.start()
    width = 2 * TILE
    eye = lax.broadcasted_iota(jnp.int32, (TILE, TILE), 0) == lax.broadcasted_iota(
        jnp.int32, (TILE, TILE), 1
    )
    for which, ref in enumerate((acts, grads)):
        for load in loads[which * LOADS:(which + 1) * LOADS]:
            load.wait()
        rest = {}
        for first in range(0, ORDER, width):
            slab = lax.dot_general(
                ref[:, first:first + width],
                ref[:, first:],
                (((0,), (0,)), ((), ())),
                preferred_element_type=F32,
            )
            for r in range(first // TILE, (first + width) // TILE):
                for c in range(r, GRID):
                    block = slab[
                        r * TILE - first:(r + 1) * TILE - first,
                        c * TILE - first:(c + 1) * TILE - first,
                    ]
                    block_b = block.astype(BF16)
                    for half in range(2):
                        piece, at = divmod(2 * WHERE[(r, c)] + half, HALVES)
                        out_ref[target_of(which, piece), at * HALF:(at + 1) * HALF] = block_b[
                            half * HALF:(half + 1) * HALF
                        ]
                        if r == c:
                            rest[(piece, at)] = jnp.sum(
                                jnp.where(eye, block - block_b.astype(F32), 0.0), axis=0, keepdims=True
                            )
        for piece in range(NZL * NY):
            lines = [rest.get((piece, at), jnp.zeros((1, TILE), F32)) for at in range(HALVES)]
            put_rest(out_ref.at[target_of(which, piece)], lines)
    gradient_load.wait()
    for shift, ref in enumerate(turn_refs):
        start = pl.multiple_of(lax.rem(y_ref[0] + shift, NY) * ORDER, ORDER)
        ref[...] = gradient[0, :, pl.ds(start, ORDER)].astype(BF16)


def target_of(which, piece):
    return (piece // NY * NXL + which) * NY + piece % NY


def put_rest(ref, lines):
    lines = lines + [jnp.zeros((1, TILE), F32)] * (REST - len(lines))
    ref[PIECE:PIECE + REST] = jnp.concatenate(lines, axis=0).astype(BF16)


def eye_of(piece, at):
    row = lax.broadcasted_iota(jnp.int32, (HALF, TILE), 0)
    return row + lax.rem(piece * HALVES + at, 2) * HALF == lax.broadcasted_iota(
        jnp.int32, (HALF, TILE), 1
    )


def sum_halves(piece, got_ref):
    count = got_ref.shape[0]
    rest = sum([got_ref[n, PIECE:].astype(F32) for n in range(1, count)], got_ref[0, PIECE:].astype(F32))
    halves = []
    for at in range(HALVES):
        s = slice(at * HALF, (at + 1) * HALF)
        total = sum([got_ref[n, s].astype(F32) for n in range(1, count)], got_ref[0, s].astype(F32))
        halves.append(total + jnp.where(eye_of(piece, at), rest[at:at + 1], 0.0))
    return halves


def put_halves(piece, out_ref, halves, more=()):
    lines = []
    for at, half in enumerate(halves):
        half_b = half.astype(BF16)
        lines.append(
            jnp.sum(jnp.where(eye_of(piece, at), half - half_b.astype(F32), 0.0), axis=0, keepdims=True)
        )
        for n in range(out_ref.shape[0]):
            out_ref[n, at * HALF:(at + 1) * HALF] = half_b
    for n in range(out_ref.shape[0]):
        put_rest(out_ref.at[n], lines + list(more))


def sum_kernel(where_ref, got_ref, *refs):
    turn_refs, (out_ref, slab_ref) = refs[:NY], refs[NY:]
    for turn, ref in enumerate(turn_refs):
        at = lax.rem(where_ref[1] + NY - turn, NY) * ROWS
        slab_ref[pl.ds(pl.multiple_of(at, ROWS), ROWS), :] = ref[...]
    put_halves(where_ref[0], out_ref, sum_halves(where_ref[0], got_ref))


def damp_kernel(all_tokens, where_ref, got_ref, slab_ref, other_ref, out_ref, slabs_ref):
    zl, rows = where_ref[2], NY * ROWS
    slabs_ref[pl.ds(pl.multiple_of(zl * rows, rows), rows), :] = slab_ref[...]
    slabs_ref[pl.ds(pl.multiple_of((1 - zl) * rows, rows), rows), :] = other_ref[...]
    piece = where_ref[0]
    halves = []
    squares = jnp.zeros((HALF, TILE), F32)
    for at, half in enumerate(sum_halves(piece, got_ref)):
        block = lax.div(piece * HALVES + at, 2)
        on_diag = functools.reduce(jnp.logical_or, [block == WHERE[(r, r)] for r in range(GRID)])
        damping = jnp.where(on_diag, DAMPING, 0.0)
        half = half / all_tokens + jnp.where(eye_of(piece, at), damping, 0.0)
        squares = squares + jnp.where(on_diag, 1.0, 2.0) * half * half
        halves.append(half)
    left = jnp.sum(jnp.sum(squares, axis=0, keepdims=True), axis=1, keepdims=True)
    left = jnp.broadcast_to(left, (1, TILE))
    terms = []
    for _ in range(TERMS):
        terms.append(left.astype(BF16).astype(F32))
        left = left - terms[-1]
    put_halves(piece, out_ref, halves, terms)


def root_kernel(packed_ref, root_ref, scaled, iterate, iterate_b, square_b, cubic_b):
    terms = sum([packed_ref[n, PIECE:].astype(F32) for n in range(NZL * NY)])[HALVES:HALVES + TERMS]
    frob = jnp.sqrt(jnp.sum(terms, axis=0, keepdims=True)[:, 0:1])
    over_frob = 1.0 / frob
    over_root = 1.0 / jnp.sqrt(frob)
    for r, c in PAIRS:
        parts = []
        for half in range(2):
            piece, at = divmod(2 * WHERE[(r, c)] + half, HALVES)
            part = packed_ref[piece, at * HALF:(at + 1) * HALF].astype(F32)
            if r == c:
                rest = packed_ref[piece, PIECE:].astype(F32)[at:at + 1]
                part = part + jnp.where(eye_of(piece, at), rest, 0.0)
            parts.append(part)
        block = (jnp.concatenate(parts, axis=0) * over_frob).astype(BF16)
        scaled[r * TILE:(r + 1) * TILE, c * TILE:(c + 1) * TILE] = block
        if r != c:
            scaled[c * TILE:(c + 1) * TILE, r * TILE:(r + 1) * TILE] = block.T
    width = 2 * TILE
    tiles = [slice(n, n + width) for n in range(0, ORDER, width)]
    for s in tiles:
        row = lax.broadcasted_iota(jnp.int32, (ORDER, width), 0)
        col = lax.broadcasted_iota(jnp.int32, (ORDER, width), 1) + s.start
        first = 1.5 * (row == col).astype(F32) - 0.5 * scaled[:, s].astype(F32)
        iterate[:, s] = first
        iterate_b[:, s] = first.astype(BF16)
    for sweep in range(SWEEPS):
        for s in tiles:
            square_b[:, s] = jnp.dot(
                iterate_b[...], iterate_b[:, s], preferred_element_type=F32
            ).astype(BF16)
        for s in tiles:
            cubic_b[:, s] = jnp.dot(
                square_b[...], scaled[:, s], preferred_element_type=F32
            ).astype(BF16)
        for s in tiles:
            new = 1.5 * iterate[:, s] - 0.5 * jnp.dot(
                cubic_b[...], iterate_b[:, s], preferred_element_type=F32
            )
            if sweep < SWEEPS - 1:
                iterate[:, s] = new
            else:
                root_ref[:, s] = (new * over_root).astype(BF16)
        if sweep < SWEEPS - 1:
            for s in tiles:
                iterate_b[:, s] = iterate[:, s].astype(BF16)

def right_kernel(where_ref, root_ref, *refs):
    slab_refs, right_refs, right = refs[:NXL], refs[NXL:NXL + NZH], refs[-1]
    zh, zl, rows = where_ref[0], where_ref[1], NY * ROWS
    cols = root_ref[:, pl.ds(pl.multiple_of(zl * (NZH * TILE), NZH * TILE), NZH * TILE)]
    for xl, ref in enumerate(slab_refs):
        done = jnp.dot(ref[...], cols, preferred_element_type=F32).astype(BF16)
        for n in range(NZL):
            right[(n * NXL + xl) * rows:(n * NXL + xl + 1) * rows] = done[n * rows:(n + 1) * rows]
    for shift, ref in enumerate(right_refs):
        at = lax.rem(zh + shift, NZH) * TILE
        ref[...] = right[:, pl.ds(pl.multiple_of(at, TILE), TILE)]


def left_kernel(where_ref, root_ref, *refs):
    right_refs, (out_ref, right) = refs[:NZH], refs[NZH:]
    for shift, ref in enumerate(right_refs):
        at = lax.rem(where_ref[0] + NZH - shift, NZH) * ZROWS
        right[pl.ds(pl.multiple_of(at, ZROWS), ZROWS), :] = ref[...]
    out_ref[...] = jnp.dot(root_ref[...], right[...], preferred_element_type=F32).astype(BF16)


def place(xl, y, block):
    return (xl * NY + y) * NBLOCK + block


def turned(x, axes, size, shift):
    return lax.ppermute(x, axes, [(n, (n + shift) % size) for n in range(size)])


def local(acts, grads_out, gradient):
    all_tokens = acts.shape[0] * NZ * NXL * NY
    y = lax.axis_index("y")
    where = jnp.stack((lax.axis_index(("zl", "y")), y, lax.axis_index("zl")))

    packed, *turns = call(
        gram_kernel,
        "gram",
        [jax.ShapeDtypeStruct((NZL * NXL * NY, PIECE + REST, TILE), BF16)]
        + [jax.ShapeDtypeStruct((ROWS, ORDER), BF16)] * NY,
        (y[None], acts, grads_out, gradient),
        specs=[SMEM] + [pl.BlockSpec(memory_space=pltpu.HBM)] * 3,
        scratch=[
            pltpu.VMEM(acts.shape, BF16),
            pltpu.VMEM(acts.shape, BF16),
            pltpu.VMEM(gradient.shape, F32),
            pltpu.SemaphoreType.DMA((2, LOADS)),
            pltpu.SemaphoreType.DMA(()),
        ],
        flops=4 * acts.shape[0] * ORDER * ORDER,
        vmem=60 << 20,
    )
    turns = [turns[0]] + [turned(turns[shift], "y", NY, shift) for shift in range(1, NY)]

    got = lax.all_to_all(packed, ("zl", "xl", "y"), 0, 0, tiled=True)
    pieces, slab = call(
        sum_kernel,
        "sum",
        [
            jax.ShapeDtypeStruct((NZH, PIECE + REST, TILE), BF16),
            jax.ShapeDtypeStruct((NY * ROWS, ORDER), BF16),
        ],
        (where, got, *turns),
        specs=[SMEM] + [VMEM] * (1 + NY),
    )
    other = turned(slab, "zl", NZL, 1)
    got = lax.all_to_all(pieces, "zh", 0, 0, tiled=True)
    pieces, slabs = call(
        functools.partial(damp_kernel, float(all_tokens)),
        "damp",
        [
            jax.ShapeDtypeStruct((NZL * NY, PIECE + REST, TILE), BF16),
            jax.ShapeDtypeStruct((NZL * NY * ROWS, ORDER), BF16),
        ],
        (where, got, slab, other),
        specs=[SMEM, VMEM, VMEM, VMEM],
    )
    cells = [(k, i) for k in range(NBLOCK) for i in range(NBLOCK)]
    slabs = [
        lax.ppermute(
            slabs,
            ("xl", "y", "xh", "c"),
            [(place(xl, k, i), place(1, i, k)) for k, i in cells],
        )
        for xl in range(NXL)
    ]
    packed = lax.all_to_all(pieces, ("zl", "y"), 0, 0, tiled=True)

    square_b = pltpu.VMEM((ORDER, ORDER), BF16)
    z_where = jnp.stack((lax.axis_index("zh"), lax.axis_index("zl")))
    right_done = jax.ShapeDtypeStruct((ZROWS, TILE), BF16)
    root = call(
        root_kernel,
        "root",
        jax.ShapeDtypeStruct((ORDER, ORDER), BF16),
        (packed,),
        scratch=[square_b, pltpu.VMEM((ORDER, ORDER), F32), square_b, square_b, square_b],
        flops=6 * SWEEPS * ORDER**3,
    )
    right_done = call(
        right_kernel,
        "right",
        [right_done] * NZH,
        (z_where, root, *slabs),
        specs=[SMEM] + [VMEM] * (1 + NXL),
        scratch=[pltpu.VMEM((ZROWS, NZH * TILE), BF16)],
        flops=2 * ORDER * ZROWS * NZH * TILE,
    )

    count = NXL * NY * NBLOCK
    right_done = [
        lax.ppermute(
            right_done[shift],
            ("zh", "xl", "y", "xh", "c"),
            [
                (zh * count + place(1, i, k), (zh + shift) % NZH * count + place(0, k, i))
                for zh in range(NZH)
                for k, i in cells
            ],
        )
        for shift in range(NZH)
    ]
    result = call(
        left_kernel,
        "left",
        jax.ShapeDtypeStruct((ORDER, TILE), BF16),
        (z_where, root, *right_done),
        specs=[SMEM] + [VMEM] * (1 + NZH),
        scratch=[pltpu.VMEM((ORDER, TILE), BF16)],
        flops=2 * ORDER * ORDER * TILE,
    )
    result = result.reshape(NZ * NXL * NY, ROWS, TILE)
    returned = lax.all_to_all(result, DP, 0, 0, tiled=True)
    returned = returned.reshape(NZH, NZL, NXL, NY, ROWS, TILE)[:, :, 0]
    return returned.transpose(3, 2, 1, 0, 4).reshape(1, ROWS, NY * NZ * TILE)


def solution(mesh):
    split = Mesh(mesh.devices.reshape(SIZES), AXES)
    block = ("xh", "c")
    in_specs = (P(DP, block), P(DP, block), P(block, DP, None))
    out_specs = P(block, DP, None)
    return jax.shard_map(local, mesh=split, in_specs=in_specs, out_specs=out_specs, check_vma=False)
```

```python
import functools

import jax
import jax.numpy as jnp
from jax import lax
from jax.experimental import pallas as pl
from jax.experimental.pallas import tpu as pltpu
from jax.sharding import Mesh, PartitionSpec as P

F32, BF16 = jnp.float32, jnp.bfloat16
SWEEPS = 2
DAMPING = 0.05
TILE = 128
VMEM_BYTES = 48 << 20

AXES = ("zh", "zl", "xl", "y", "xh", "c")
SIZES = (4, 2, 2, 4, 2, 2)
NZH, NZL, NXL, NY, NXH, NC = SIZES
NZ, NBLOCK = NZH * NZL, NXH * NC
DP = ("zh", "zl", "xl", "y")

ORDER = 1024
GRID = ORDER // TILE
PAIRS = [(r, c) for r in range(GRID) for c in range(r, GRID)]
WHERE = {pair: n for n, pair in enumerate(PAIRS)}

HALF = TILE // 2
HALVES = 2 * len(PAIRS) // (NZL * NY)
PIECE = HALVES * HALF
REST = 16
ROWS = 16
TERMS = 3
LOADS = 4
ZROWS = NZL * NXL * NY * ROWS


def call(kernel, name, out_shape, args, specs=None, scratch=(), flops=0, vmem=VMEM_BYTES):
    extra = {} if specs is None else {"in_specs": specs}
    return pl.pallas_call(
        kernel,
        out_shape=out_shape,
        scratch_shapes=list(scratch),
        compiler_params=pltpu.CompilerParams(vmem_limit_bytes=vmem),
        cost_estimate=pl.CostEstimate(flops=flops, bytes_accessed=4 << 20, transcendentals=0),
        name=name,
        **extra,
    )(*args)


SMEM = pl.BlockSpec(memory_space=pltpu.SMEM)
VMEM = pl.BlockSpec(memory_space=pltpu.VMEM)


def gram_kernel(y_ref, acts_ref, grads_ref, gradient_ref, out_ref, *refs):
    turn_refs, (acts, grads, gradient, sems, gradient_sem) = refs[:NY], refs[NY:]
    rows = acts.shape[0] // LOADS
    loads = []
    for which, (far, near) in enumerate(((acts_ref, acts), (grads_ref, grads))):
        for n in range(LOADS):
            part = pl.ds(n * rows, rows)
            loads.append(pltpu.make_async_copy(far.at[part], near.at[part], sems.at[which, n]))
            loads[-1].start()
    gradient_load = pltpu.make_async_copy(gradient_ref, gradient, gradient_sem)
    gradient_load.start()
    width = 2 * TILE
    eye = lax.broadcasted_iota(jnp.int32, (TILE, TILE), 0) == lax.broadcasted_iota(
        jnp.int32, (TILE, TILE), 1
    )
    for which, ref in enumerate((acts, grads)):
        for load in loads[which * LOADS:(which + 1) * LOADS]:
            load.wait()
        rest = {}
        for first in range(0, ORDER, width):
            slab = lax.dot_general(
                ref[:, first:first + width],
                ref[:, first:],
                (((0,), (0,)), ((), ())),
                preferred_element_type=F32,
            )
            for r in range(first // TILE, (first + width) // TILE):
                for c in range(r, GRID):
                    block = slab[
                        r * TILE - first:(r + 1) * TILE - first,
                        c * TILE - first:(c + 1) * TILE - first,
                    ]
                    block_b = block.astype(BF16)
                    for half in range(2):
                        piece, at = divmod(2 * WHERE[(r, c)] + half, HALVES)
                        out_ref[target_of(which, piece), at * HALF:(at + 1) * HALF] = block_b[
                            half * HALF:(half + 1) * HALF
                        ]
                        if r == c:
                            rest[(piece, at)] = jnp.sum(
                                jnp.where(eye, block - block_b.astype(F32), 0.0), axis=0, keepdims=True
                            )
        for piece in range(NZL * NY):
            lines = [rest.get((piece, at), jnp.zeros((1, TILE), F32)) for at in range(HALVES)]
            put_rest(out_ref.at[target_of(which, piece)], lines)
    gradient_load.wait()
    for shift, ref in enumerate(turn_refs):
        start = pl.multiple_of(lax.rem(y_ref[0] + shift, NY) * ORDER, ORDER)
        ref[...] = gradient[0, :, pl.ds(start, ORDER)].astype(BF16)


def target_of(which, piece):
    return (piece // NY * NXL + which) * NY + piece % NY


def put_rest(ref, lines):
    lines = lines + [jnp.zeros((1, TILE), F32)] * (REST - len(lines))
    ref[PIECE:PIECE + REST] = jnp.concatenate(lines, axis=0).astype(BF16)


def eye_of(piece, at):
    row = lax.broadcasted_iota(jnp.int32, (HALF, TILE), 0)
    return row + lax.rem(piece * HALVES + at, 2) * HALF == lax.broadcasted_iota(
        jnp.int32, (HALF, TILE), 1
    )


def sum_halves(piece, got_ref):
    count = got_ref.shape[0]
    rest = sum([got_ref[n, PIECE:].astype(F32) for n in range(1, count)], got_ref[0, PIECE:].astype(F32))
    halves = []
    for at in range(HALVES):
        s = slice(at * HALF, (at + 1) * HALF)
        total = sum([got_ref[n, s].astype(F32) for n in range(1, count)], got_ref[0, s].astype(F32))
        halves.append(total + jnp.where(eye_of(piece, at), rest[at:at + 1], 0.0))
    return halves


def put_halves(piece, out_ref, halves, more=()):
    lines = []
    for at, half in enumerate(halves):
        half_b = half.astype(BF16)
        lines.append(
            jnp.sum(jnp.where(eye_of(piece, at), half - half_b.astype(F32), 0.0), axis=0, keepdims=True)
        )
        for n in range(out_ref.shape[0]):
            out_ref[n, at * HALF:(at + 1) * HALF] = half_b
    for n in range(out_ref.shape[0]):
        put_rest(out_ref.at[n], lines + list(more))


def sum_kernel(where_ref, got_ref, *refs):
    turn_refs, (out_ref, slab_ref) = refs[:NY], refs[NY:]
    for turn, ref in enumerate(turn_refs):
        at = lax.rem(where_ref[1] + NY - turn, NY) * ROWS
        slab_ref[pl.ds(pl.multiple_of(at, ROWS), ROWS), :] = ref[...]
    put_halves(where_ref[0], out_ref, sum_halves(where_ref[0], got_ref))


def damp_kernel(all_tokens, where_ref, got_ref, other_ref, out_ref):
    piece = where_ref[0]
    halves = []
    squares = jnp.zeros((HALF, TILE), F32)
    for at, half in enumerate(sum_halves(piece, got_ref)):
        block = lax.div(piece * HALVES + at, 2)
        on_diag = functools.reduce(jnp.logical_or, [block == WHERE[(r, r)] for r in range(GRID)])
        damping = jnp.where(on_diag, DAMPING, 0.0)
        half = half / all_tokens + jnp.where(eye_of(piece, at), damping, 0.0)
        squares = squares + jnp.where(on_diag, 1.0, 2.0) * half * half
        halves.append(half)
    left = jnp.sum(jnp.sum(squares, axis=0, keepdims=True), axis=1, keepdims=True)
    left = jnp.broadcast_to(left, (1, TILE))
    terms = []
    for _ in range(TERMS):
        terms.append(left.astype(BF16).astype(F32))
        left = left - terms[-1]
    put_halves(piece, out_ref, halves, terms)


def scale_kernel(where_ref, packed_ref, slab_ref, other_ref, scaled, over_ref, slabs_ref):
    zl, rows = where_ref[2], NY * ROWS
    slabs_ref[pl.ds(pl.multiple_of(zl * rows, rows), rows), :] = slab_ref[...]
    slabs_ref[pl.ds(pl.multiple_of((1 - zl) * rows, rows), rows), :] = other_ref[...]
    terms = sum([packed_ref[n, PIECE:].astype(F32) for n in range(NZL * NY)])[HALVES:HALVES + TERMS]
    frob = jnp.sqrt(jnp.sum(terms, axis=0, keepdims=True)[:, 0:1])
    over_frob = 1.0 / frob
    over_ref[...] = jnp.broadcast_to(1.0 / jnp.sqrt(frob), over_ref.shape)
    for r, c in PAIRS:
        parts = []
        for half in range(2):
            piece, at = divmod(2 * WHERE[(r, c)] + half, HALVES)
            part = packed_ref[piece, at * HALF:(at + 1) * HALF].astype(F32)
            if r == c:
                rest = packed_ref[piece, PIECE:].astype(F32)[at:at + 1]
                part = part + jnp.where(eye_of(piece, at), rest, 0.0)
            parts.append(part)
        block = (jnp.concatenate(parts, axis=0) * over_frob).astype(BF16)
        scaled[r * TILE:(r + 1) * TILE, c * TILE:(c + 1) * TILE] = block
        if r != c:
            scaled[c * TILE:(c + 1) * TILE, r * TILE:(r + 1) * TILE] = block.T


def root_kernel(scaled, over_ref, root_ref, iterate, iterate_b, square_b, cubic_b):
    over_root = over_ref[0:1, 0:1]
    width = 2 * TILE
    tiles = [slice(n, n + width) for n in range(0, ORDER, width)]
    for s in tiles:
        row = lax.broadcasted_iota(jnp.int32, (ORDER, width), 0)
        col = lax.broadcasted_iota(jnp.int32, (ORDER, width), 1) + s.start
        first = 1.5 * (row == col).astype(F32) - 0.5 * scaled[:, s].astype(F32)
        iterate[:, s] = first
        iterate_b[:, s] = first.astype(BF16)
    for sweep in range(SWEEPS):
        for s in tiles:
            square_b[:, s] = jnp.dot(
                iterate_b[...], iterate_b[:, s], preferred_element_type=F32
            ).astype(BF16)
        for s in tiles:
            cubic_b[:, s] = jnp.dot(
                square_b[...], scaled[:, s], preferred_element_type=F32
            ).astype(BF16)
        for s in tiles:
            new = 1.5 * iterate[:, s] - 0.5 * jnp.dot(
                cubic_b[...], iterate_b[:, s], preferred_element_type=F32
            )
            if sweep < SWEEPS - 1:
                iterate[:, s] = new
            else:
                root_ref[:, s] = (new * over_root).astype(BF16)
        if sweep < SWEEPS - 1:
            for s in tiles:
                iterate_b[:, s] = iterate[:, s].astype(BF16)

def right_kernel(where_ref, root_ref, *refs):
    slab_refs, right_refs, right = refs[:NXL], refs[NXL:NXL + NZH], refs[-1]
    zh, zl, rows = where_ref[0], where_ref[1], NY * ROWS
    cols = root_ref[:, pl.ds(pl.multiple_of(zl * (NZH * TILE), NZH * TILE), NZH * TILE)]
    for xl, ref in enumerate(slab_refs):
        done = jnp.dot(ref[...], cols, preferred_element_type=F32).astype(BF16)
        for n in range(NZL):
            right[(n * NXL + xl) * rows:(n * NXL + xl + 1) * rows] = done[n * rows:(n + 1) * rows]
    for shift, ref in enumerate(right_refs):
        at = lax.rem(zh + shift, NZH) * TILE
        ref[...] = right[:, pl.ds(pl.multiple_of(at, TILE), TILE)]


def left_kernel(where_ref, root_ref, *refs):
    right_refs, (out_ref, right) = refs[:NZH], refs[NZH:]
    for shift, ref in enumerate(right_refs):
        at = lax.rem(where_ref[0] + NZH - shift, NZH) * ZROWS
        right[pl.ds(pl.multiple_of(at, ZROWS), ZROWS), :] = ref[...]
    out_ref[...] = jnp.dot(root_ref[...], right[...], preferred_element_type=F32).astype(BF16)


def place(xl, y, block):
    return (xl * NY + y) * NBLOCK + block


def turned(x, axes, size, shift):
    return lax.ppermute(x, axes, [(n, (n + shift) % size) for n in range(size)])


def local(acts, grads_out, gradient):
    all_tokens = acts.shape[0] * NZ * NXL * NY
    y = lax.axis_index("y")
    where = jnp.stack((lax.axis_index(("zl", "y")), y, lax.axis_index("zl")))

    packed, *turns = call(
        gram_kernel,
        "gram",
        [jax.ShapeDtypeStruct((NZL * NXL * NY, PIECE + REST, TILE), BF16)]
        + [jax.ShapeDtypeStruct((ROWS, ORDER), BF16)] * NY,
        (y[None], acts, grads_out, gradient),
        specs=[SMEM] + [pl.BlockSpec(memory_space=pltpu.HBM)] * 3,
        scratch=[
            pltpu.VMEM(acts.shape, BF16),
            pltpu.VMEM(acts.shape, BF16),
            pltpu.VMEM(gradient.shape, F32),
            pltpu.SemaphoreType.DMA((2, LOADS)),
            pltpu.SemaphoreType.DMA(()),
        ],
        flops=4 * acts.shape[0] * ORDER * ORDER,
        vmem=60 << 20,
    )
    turns = [turns[0]] + [turned(turns[shift], "y", NY, shift) for shift in range(1, NY)]

    got = lax.all_to_all(packed, ("zl", "xl", "y"), 0, 0, tiled=True)
    pieces, slab = call(
        sum_kernel,
        "sum",
        [
            jax.ShapeDtypeStruct((NZH, PIECE + REST, TILE), BF16),
            jax.ShapeDtypeStruct((NY * ROWS, ORDER), BF16),
        ],
        (where, got, *turns),
        specs=[SMEM] + [VMEM] * (1 + NY),
    )
    other = turned(slab, "zl", NZL, 1)
    got = lax.all_to_all(pieces, "zh", 0, 0, tiled=True)
    pieces = call(
        functools.partial(damp_kernel, float(all_tokens)),
        "damp",
        jax.ShapeDtypeStruct((NZL * NY, PIECE + REST, TILE), BF16),
        (where, got, other),
        specs=[SMEM, VMEM, pl.BlockSpec(memory_space=pl.ANY)],
    )
    packed = lax.all_to_all(pieces, ("zl", "y"), 0, 0, tiled=True)

    scaled, over_root, slabs = call(
        scale_kernel,
        "scale",
        [
            jax.ShapeDtypeStruct((ORDER, ORDER), BF16),
            jax.ShapeDtypeStruct((8, TILE), F32),
            jax.ShapeDtypeStruct((NZL * NY * ROWS, ORDER), BF16),
        ],
        (where, packed, slab, other),
        specs=[SMEM, VMEM, VMEM, VMEM],
    )
    cells = [(k, i) for k in range(NBLOCK) for i in range(NBLOCK)]
    slabs = [
        lax.ppermute(
            slabs,
            ("xl", "y", "xh", "c"),
            [(place(xl, k, i), place(1, i, k)) for k, i in cells],
        )
        for xl in range(NXL)
    ]

    square_b = pltpu.VMEM((ORDER, ORDER), BF16)
    z_where = jnp.stack((lax.axis_index("zh"), lax.axis_index("zl")))
    right_done = jax.ShapeDtypeStruct((ZROWS, TILE), BF16)
    root = call(
        root_kernel,
        "root",
        jax.ShapeDtypeStruct((ORDER, ORDER), BF16),
        (scaled, over_root),
        scratch=[pltpu.VMEM((ORDER, ORDER), F32), square_b, square_b, square_b],
        flops=6 * SWEEPS * ORDER**3,
    )
    right_done = call(
        right_kernel,
        "right",
        [right_done] * NZH,
        (z_where, root, *slabs),
        specs=[SMEM] + [VMEM] * (1 + NXL),
        scratch=[pltpu.VMEM((ZROWS, NZH * TILE), BF16)],
        flops=2 * ORDER * ZROWS * NZH * TILE,
    )

    count = NXL * NY * NBLOCK
    right_done = [
        lax.ppermute(
            right_done[shift],
            ("zh", "xl", "y", "xh", "c"),
            [
                (zh * count + place(1, i, k), (zh + shift) % NZH * count + place(0, k, i))
                for zh in range(NZH)
                for k, i in cells
            ],
        )
        for shift in range(NZH)
    ]
    result = call(
        left_kernel,
        "left",
        jax.ShapeDtypeStruct((ORDER, TILE), BF16),
        (z_where, root, *right_done),
        specs=[SMEM] + [VMEM] * (1 + NZH),
        scratch=[pltpu.VMEM((ORDER, TILE), BF16)],
        flops=2 * ORDER * ORDER * TILE,
    )
    result = result.reshape(NZ * NXL * NY, ROWS, TILE)
    returned = lax.all_to_all(result, DP, 0, 0, tiled=True)
    returned = returned.reshape(NZH, NZL, NXL, NY, ROWS, TILE)[:, :, 0]
    return returned.transpose(3, 2, 1, 0, 4).reshape(1, ROWS, NY * NZ * TILE)


def solution(mesh):
    split = Mesh(mesh.devices.reshape(SIZES), AXES)
    block = ("xh", "c")
    in_specs = (P(DP, block), P(DP, block), P(block, DP, None))
    out_specs = P(block, DP, None)
    return jax.shard_map(local, mesh=split, in_specs=in_specs, out_specs=out_specs, check_vma=False)
```

```python
import functools

import jax
import jax.numpy as jnp
from jax import lax
from jax.experimental import pallas as pl
from jax.experimental.pallas import tpu as pltpu
from jax.sharding import Mesh, PartitionSpec as P

F32, BF16 = jnp.float32, jnp.bfloat16
SWEEPS = 2
DAMPING = 0.05
TILE = 128
VMEM_BYTES = 48 << 20

AXES = ("zh", "zl", "xl", "y", "xh", "c")
SIZES = (4, 2, 2, 4, 2, 2)
NZH, NZL, NXL, NY, NXH, NC = SIZES
NZ, NBLOCK = NZH * NZL, NXH * NC
DP = ("zh", "zl", "xl", "y")

ORDER = 1024
GRID = ORDER // TILE
PAIRS = [(r, c) for r in range(GRID) for c in range(r, GRID)]
WHERE = {pair: n for n, pair in enumerate(PAIRS)}

HALF = TILE // 2
HALVES = 2 * len(PAIRS) // (NZL * NY)
PIECE = HALVES * HALF
REST = 16
ROWS = 16
TERMS = 3
LOADS = 4
ZROWS = NZL * NXL * NY * ROWS


def call(kernel, name, out_shape, args, specs=None, scratch=(), flops=0, vmem=VMEM_BYTES):
    extra = {} if specs is None else {"in_specs": specs}
    return pl.pallas_call(
        kernel,
        out_shape=out_shape,
        scratch_shapes=list(scratch),
        compiler_params=pltpu.CompilerParams(vmem_limit_bytes=vmem),
        cost_estimate=pl.CostEstimate(flops=flops, bytes_accessed=4 << 20, transcendentals=0),
        name=name,
        **extra,
    )(*args)


SMEM = pl.BlockSpec(memory_space=pltpu.SMEM)
VMEM = pl.BlockSpec(memory_space=pltpu.VMEM)


def flip(block):
    return block // NC + block % NC * NXH


def partner(block, y):
    return flip(block) ^ y


def flip_scalar(block):
    return lax.div(block, NC) + lax.rem(block, NC) * NXH


def gram_kernel(y_ref, acts_ref, grads_ref, gradient_ref, out_ref, *refs):
    turn_refs, (acts, grads, gradient, sems, gradient_sem) = refs[:NY], refs[NY:]
    rows = acts.shape[0] // LOADS
    loads = []
    for which, (far, near) in enumerate(((acts_ref, acts), (grads_ref, grads))):
        for n in range(LOADS):
            part = pl.ds(n * rows, rows)
            loads.append(pltpu.make_async_copy(far.at[part], near.at[part], sems.at[which, n]))
            loads[-1].start()
    gradient_load = pltpu.make_async_copy(gradient_ref, gradient, gradient_sem)
    gradient_load.start()
    width = 2 * TILE
    eye = lax.broadcasted_iota(jnp.int32, (TILE, TILE), 0) == lax.broadcasted_iota(
        jnp.int32, (TILE, TILE), 1
    )
    for which, ref in enumerate((acts, grads)):
        for load in loads[which * LOADS:(which + 1) * LOADS]:
            load.wait()
        rest = {}
        for first in range(0, ORDER, width):
            slab = lax.dot_general(
                ref[:, first:first + width],
                ref[:, first:],
                (((0,), (0,)), ((), ())),
                preferred_element_type=F32,
            )
            for r in range(first // TILE, (first + width) // TILE):
                for c in range(r, GRID):
                    block = slab[
                        r * TILE - first:(r + 1) * TILE - first,
                        c * TILE - first:(c + 1) * TILE - first,
                    ]
                    block_b = block.astype(BF16)
                    for half in range(2):
                        piece, at = divmod(2 * WHERE[(r, c)] + half, HALVES)
                        out_ref[target_of(which, piece), at * HALF:(at + 1) * HALF] = block_b[
                            half * HALF:(half + 1) * HALF
                        ]
                        if r == c:
                            rest[(piece, at)] = jnp.sum(
                                jnp.where(eye, block - block_b.astype(F32), 0.0), axis=0, keepdims=True
                            )
        for piece in range(NZL * NY):
            lines = [rest.get((piece, at), jnp.zeros((1, TILE), F32)) for at in range(HALVES)]
            put_rest(out_ref.at[target_of(which, piece)], lines)
    gradient_load.wait()
    for shift, ref in enumerate(turn_refs):
        block = flip_scalar(jnp.bitwise_xor(y_ref[1], lax.rem(y_ref[0] + shift, NY)))
        start = pl.multiple_of(block * ORDER, ORDER)
        ref[...] = gradient[0, :, pl.ds(start, ORDER)].astype(BF16)


def target_of(which, piece):
    return (piece // NY * NXL + which) * NY + piece % NY


def put_rest(ref, lines):
    lines = lines + [jnp.zeros((1, TILE), F32)] * (REST - len(lines))
    ref[PIECE:PIECE + REST] = jnp.concatenate(lines, axis=0).astype(BF16)


def eye_of(piece, at):
    row = lax.broadcasted_iota(jnp.int32, (HALF, TILE), 0)
    return row + lax.rem(piece * HALVES + at, 2) * HALF == lax.broadcasted_iota(
        jnp.int32, (HALF, TILE), 1
    )


def sum_halves(piece, got_ref):
    count = got_ref.shape[0]
    rest = sum([got_ref[n, PIECE:].astype(F32) for n in range(1, count)], got_ref[0, PIECE:].astype(F32))
    halves = []
    for at in range(HALVES):
        s = slice(at * HALF, (at + 1) * HALF)
        total = sum([got_ref[n, s].astype(F32) for n in range(1, count)], got_ref[0, s].astype(F32))
        halves.append(total + jnp.where(eye_of(piece, at), rest[at:at + 1], 0.0))
    return halves


def put_halves(piece, out_ref, halves, more=()):
    lines = []
    for at, half in enumerate(halves):
        half_b = half.astype(BF16)
        lines.append(
            jnp.sum(jnp.where(eye_of(piece, at), half - half_b.astype(F32), 0.0), axis=0, keepdims=True)
        )
        for n in range(out_ref.shape[0]):
            out_ref[n, at * HALF:(at + 1) * HALF] = half_b
    for n in range(out_ref.shape[0]):
        put_rest(out_ref.at[n], lines + list(more))


def sum_kernel(where_ref, got_ref, *refs):
    turn_refs, (out_ref, slab_ref) = refs[:NY], refs[NY:]
    for turn, ref in enumerate(turn_refs):
        at = lax.rem(where_ref[1] + NY - turn, NY) * ROWS
        slab_ref[pl.ds(pl.multiple_of(at, ROWS), ROWS), :] = ref[...]
    put_halves(where_ref[0], out_ref, sum_halves(where_ref[0], got_ref))


def damp_kernel(all_tokens, where_ref, got_ref, slab_ref, other_ref, out_ref, slabs_ref):
    zl, rows = where_ref[2], NY * ROWS
    slabs_ref[pl.ds(pl.multiple_of(zl * rows, rows), rows), :] = slab_ref[...]
    slabs_ref[pl.ds(pl.multiple_of((1 - zl) * rows, rows), rows), :] = other_ref[...]
    piece = where_ref[0]
    halves = []
    squares = jnp.zeros((HALF, TILE), F32)
    for at, half in enumerate(sum_halves(piece, got_ref)):
        block = lax.div(piece * HALVES + at, 2)
        on_diag = functools.reduce(jnp.logical_or, [block == WHERE[(r, r)] for r in range(GRID)])
        damping = jnp.where(on_diag, DAMPING, 0.0)
        half = half / all_tokens + jnp.where(eye_of(piece, at), damping, 0.0)
        squares = squares + jnp.where(on_diag, 1.0, 2.0) * half * half
        halves.append(half)
    left = jnp.sum(jnp.sum(squares, axis=0, keepdims=True), axis=1, keepdims=True)
    left = jnp.broadcast_to(left, (1, TILE))
    terms = []
    for _ in range(TERMS):
        terms.append(left.astype(BF16).astype(F32))
        left = left - terms[-1]
    put_halves(piece, out_ref, halves, terms)


def root_kernel(packed_ref, root_ref, scaled, iterate, iterate_b, square_b, cubic_b):
    terms = sum([packed_ref[n, PIECE:].astype(F32) for n in range(NZL * NY)])[HALVES:HALVES + TERMS]
    frob = jnp.sqrt(jnp.sum(terms, axis=0, keepdims=True)[:, 0:1])
    over_frob = 1.0 / frob
    over_root = 1.0 / jnp.sqrt(frob)
    for r, c in PAIRS:
        parts = []
        for half in range(2):
            piece, at = divmod(2 * WHERE[(r, c)] + half, HALVES)
            part = packed_ref[piece, at * HALF:(at + 1) * HALF].astype(F32)
            if r == c:
                rest = packed_ref[piece, PIECE:].astype(F32)[at:at + 1]
                part = part + jnp.where(eye_of(piece, at), rest, 0.0)
            parts.append(part)
        block = (jnp.concatenate(parts, axis=0) * over_frob).astype(BF16)
        scaled[r * TILE:(r + 1) * TILE, c * TILE:(c + 1) * TILE] = block
        if r != c:
            scaled[c * TILE:(c + 1) * TILE, r * TILE:(r + 1) * TILE] = block.T
    width = 2 * TILE
    tiles = [slice(n, n + width) for n in range(0, ORDER, width)]
    for s in tiles:
        row = lax.broadcasted_iota(jnp.int32, (ORDER, width), 0)
        col = lax.broadcasted_iota(jnp.int32, (ORDER, width), 1) + s.start
        first = 1.5 * (row == col).astype(F32) - 0.5 * scaled[:, s].astype(F32)
        iterate[:, s] = first
        iterate_b[:, s] = first.astype(BF16)
    for sweep in range(SWEEPS):
        for s in tiles:
            square_b[:, s] = jnp.dot(
                iterate_b[...], iterate_b[:, s], preferred_element_type=F32
            ).astype(BF16)
        for s in tiles:
            cubic_b[:, s] = jnp.dot(
                square_b[...], scaled[:, s], preferred_element_type=F32
            ).astype(BF16)
        for s in tiles:
            new = 1.5 * iterate[:, s] - 0.5 * jnp.dot(
                cubic_b[...], iterate_b[:, s], preferred_element_type=F32
            )
            if sweep < SWEEPS - 1:
                iterate[:, s] = new
            else:
                root_ref[:, s] = (new * over_root).astype(BF16)
        if sweep < SWEEPS - 1:
            for s in tiles:
                iterate_b[:, s] = iterate[:, s].astype(BF16)

def right_kernel(where_ref, root_ref, *refs):
    slab_refs, right_refs, right = refs[:NXL], refs[NXL:NXL + NZH], refs[-1]
    zh, zl, rows = where_ref[0], where_ref[1], NY * ROWS
    cols = root_ref[:, pl.ds(pl.multiple_of(zl * (NZH * TILE), NZH * TILE), NZH * TILE)]
    for xl, ref in enumerate(slab_refs):
        done = jnp.dot(ref[...], cols, preferred_element_type=F32).astype(BF16)
        for n in range(NZL):
            right[(n * NXL + xl) * rows:(n * NXL + xl + 1) * rows] = done[n * rows:(n + 1) * rows]
    for shift, ref in enumerate(right_refs):
        at = lax.rem(zh + shift, NZH) * TILE
        ref[...] = right[:, pl.ds(pl.multiple_of(at, TILE), TILE)]


def left_kernel(where_ref, root_ref, *refs):
    right_refs, (out_ref, right) = refs[:NZH], refs[NZH:]
    for shift, ref in enumerate(right_refs):
        at = lax.rem(where_ref[0] + NZH - shift, NZH) * ZROWS
        right[pl.ds(pl.multiple_of(at, ZROWS), ZROWS), :] = ref[...]
    out_ref[...] = jnp.dot(root_ref[...], right[...], preferred_element_type=F32).astype(BF16)


def place_kernel(block_ref, got_ref, out_ref):
    for k in range(NBLOCK):
        y = jnp.bitwise_xor(block_ref[0], flip(k))
        for z in range(NZ):
            at = k * ORDER + z % NZL * (NZH * TILE) + z // NZL * TILE
            out_ref[0, :, at:at + TILE] = got_ref[z * NXL * NY + y]


def place(xl, y, block):
    return (xl * NY + y) * NBLOCK + block


def turned(x, axes, size, shift):
    return lax.ppermute(x, axes, [(n, (n + shift) % size) for n in range(size)])


def local(acts, grads_out, gradient):
    all_tokens = acts.shape[0] * NZ * NXL * NY
    y = lax.axis_index("y")
    block = lax.axis_index(("xh", "c"))
    where = jnp.stack((lax.axis_index(("zl", "y")), y, lax.axis_index("zl")))

    packed, *turns = call(
        gram_kernel,
        "gram",
        [jax.ShapeDtypeStruct((NZL * NXL * NY, PIECE + REST, TILE), BF16)]
        + [jax.ShapeDtypeStruct((ROWS, ORDER), BF16)] * NY,
        (jnp.stack((y, block)), acts, grads_out, gradient),
        specs=[SMEM] + [pl.BlockSpec(memory_space=pltpu.HBM)] * 3,
        scratch=[
            pltpu.VMEM(acts.shape, BF16),
            pltpu.VMEM(acts.shape, BF16),
            pltpu.VMEM(gradient.shape, F32),
            pltpu.SemaphoreType.DMA((2, LOADS)),
            pltpu.SemaphoreType.DMA(()),
        ],
        flops=4 * acts.shape[0] * ORDER * ORDER,
        vmem=60 << 20,
    )
    turns = [turns[0]] + [turned(turns[shift], "y", NY, shift) for shift in range(1, NY)]

    got = lax.all_to_all(packed, ("zl", "xl", "y"), 0, 0, tiled=True)
    pieces, slab = call(
        sum_kernel,
        "sum",
        [
            jax.ShapeDtypeStruct((NZH, PIECE + REST, TILE), BF16),
            jax.ShapeDtypeStruct((NY * ROWS, ORDER), BF16),
        ],
        (where, got, *turns),
        specs=[SMEM] + [VMEM] * (1 + NY),
    )
    other = turned(slab, "zl", NZL, 1)
    got = lax.all_to_all(pieces, "zh", 0, 0, tiled=True)
    pieces, slabs = call(
        functools.partial(damp_kernel, float(all_tokens)),
        "damp",
        [
            jax.ShapeDtypeStruct((NZL * NY, PIECE + REST, TILE), BF16),
            jax.ShapeDtypeStruct((NZL * NY * ROWS, ORDER), BF16),
        ],
        (where, got, slab, other),
        specs=[SMEM, VMEM, VMEM, VMEM],
    )
    cells = [(partner(k, y), k, y) for k in range(NBLOCK) for y in range(NY)]
    slabs = [
        lax.ppermute(
            slabs,
            ("xl", "y", "xh", "c"),
            [(place(xl, y, i), place(1, y, k)) for i, k, y in cells],
        )
        for xl in range(NXL)
    ]
    packed = lax.all_to_all(pieces, ("zl", "y"), 0, 0, tiled=True)

    square_b = pltpu.VMEM((ORDER, ORDER), BF16)
    z_where = jnp.stack((lax.axis_index("zh"), lax.axis_index("zl")))
    right_done = jax.ShapeDtypeStruct((ZROWS, TILE), BF16)
    root = call(
        root_kernel,
        "root",
        jax.ShapeDtypeStruct((ORDER, ORDER), BF16),
        (packed,),
        scratch=[square_b, pltpu.VMEM((ORDER, ORDER), F32), square_b, square_b, square_b],
        flops=6 * SWEEPS * ORDER**3,
    )
    right_done = call(
        right_kernel,
        "right",
        [right_done] * NZH,
        (z_where, root, *slabs),
        specs=[SMEM] + [VMEM] * (1 + NXL),
        scratch=[pltpu.VMEM((ZROWS, NZH * TILE), BF16)],
        flops=2 * ORDER * ZROWS * NZH * TILE,
    )

    count = NXL * NY * NBLOCK
    right_done = [
        lax.ppermute(
            right_done[shift],
            ("zh", "xl", "y", "xh", "c"),
            [
                (zh * count + place(1, y, k), (zh + shift) % NZH * count + place(0, y, i))
                for zh in range(NZH)
                for i, k, y in cells
            ],
        )
        for shift in range(NZH)
    ]
    result = call(
        left_kernel,
        "left",
        jax.ShapeDtypeStruct((ORDER, TILE), BF16),
        (z_where, root, *right_done),
        specs=[SMEM] + [VMEM] * (1 + NZH),
        scratch=[pltpu.VMEM((ORDER, TILE), BF16)],
        flops=2 * ORDER * ORDER * TILE,
    )
    result = result.reshape(NZ * NXL * NY, ROWS, TILE)
    returned = lax.all_to_all(result, DP, 0, 0, tiled=True)
    return call(
        place_kernel,
        "place",
        jax.ShapeDtypeStruct((1, ROWS, NBLOCK * ORDER), BF16),
        (block[None], returned),
        specs=[SMEM, VMEM],
    )


def solution(mesh):
    split = Mesh(mesh.devices.reshape(SIZES), AXES)
    block = ("xh", "c")
    in_specs = (P(DP, block), P(DP, block), P(block, DP, None))
    out_specs = P(block, DP, None)
    return jax.shard_map(local, mesh=split, in_specs=in_specs, out_specs=out_specs, check_vma=False)
```

```python
import functools

import jax
import jax.numpy as jnp
from jax import lax
from jax.experimental import pallas as pl
from jax.experimental.pallas import tpu as pltpu
from jax.sharding import Mesh, PartitionSpec as P

F32, BF16 = jnp.float32, jnp.bfloat16
SWEEPS = 2
DAMPING = 0.05
TILE = 128
VMEM_BYTES = 48 << 20

AXES = ("zh", "zl", "xl", "y", "xh", "c")
SIZES = (4, 2, 2, 4, 2, 2)
NZH, NZL, NXL, NY, NXH, NC = SIZES
NZ, NBLOCK = NZH * NZL, NXH * NC
DP = ("zh", "zl", "xl", "y")

ORDER = 1024
GRID = ORDER // TILE
PAIRS = [(r, c) for r in range(GRID) for c in range(r, GRID)]
WHERE = {pair: n for n, pair in enumerate(PAIRS)}

HALF = TILE // 2
HALVES = 2 * len(PAIRS) // (NZL * NY)
PIECE = HALVES * HALF
REST = 16
ROWS = 16
TERMS = 3
SHIFTS = (2, 1, 3, 0)
LOADS = 4
ZROWS = NZL * NXL * NY * ROWS


def call(
    kernel, name, out_shape, args, specs=None, out_specs=None, scratch=(), flops=0, vmem=VMEM_BYTES
):
    extra = {} if specs is None else {"in_specs": specs}
    if out_specs is not None:
        extra["out_specs"] = out_specs
    return pl.pallas_call(
        kernel,
        out_shape=out_shape,
        scratch_shapes=list(scratch),
        compiler_params=pltpu.CompilerParams(vmem_limit_bytes=vmem),
        cost_estimate=pl.CostEstimate(flops=flops, bytes_accessed=4 << 20, transcendentals=0),
        name=name,
        **extra,
    )(*args)


HBM = pl.BlockSpec(memory_space=pltpu.HBM)
VMEM = pl.BlockSpec(memory_space=pltpu.VMEM)


def flip(block):
    return block // NC + block % NC * NXH


def partner(block, y):
    return flip(block) ^ y


def flip_scalar(block):
    return lax.div(block, NC) + lax.rem(block, NC) * NXH


def block_here():
    return lax.axis_index("xh") * NC + lax.axis_index("c")


def piece_here():
    return lax.axis_index("zl") * NY + lax.axis_index("y")


def gram_kernel(acts_ref, grads_ref, gradient_ref, out_ref, *refs):
    turn_refs, (acts, grads, gradient, packed, sems, gradient_sem, out_sems) = refs[:NY], refs[NY:]
    rows = acts.shape[0] // LOADS
    loads = []
    for which, (far, near) in enumerate(((acts_ref, acts), (grads_ref, grads))):
        for n in range(LOADS):
            part = pl.ds(n * rows, rows)
            loads.append(pltpu.make_async_copy(far.at[part], near.at[part], sems.at[which, n]))
            loads[-1].start()
    gradient_load = pltpu.make_async_copy(gradient_ref, gradient, gradient_sem)
    gradient_load.start()
    width = 2 * TILE
    eye = lax.broadcasted_iota(jnp.int32, (TILE, TILE), 0) == lax.broadcasted_iota(
        jnp.int32, (TILE, TILE), 1
    )
    stores = []
    for which, ref in enumerate((acts, grads)):
        for load in loads[which * LOADS:(which + 1) * LOADS]:
            load.wait()
        rest = {}
        for first in range(0, ORDER, width):
            slab = lax.dot_general(
                ref[:, first:first + width],
                ref[:, first:],
                (((0,), (0,)), ((), ())),
                preferred_element_type=F32,
            )
            for r in range(first // TILE, (first + width) // TILE):
                for c in range(r, GRID):
                    block = slab[
                        r * TILE - first:(r + 1) * TILE - first,
                        c * TILE - first:(c + 1) * TILE - first,
                    ]
                    block_b = block.astype(BF16)
                    for half in range(2):
                        piece, at = divmod(2 * WHERE[(r, c)] + half, HALVES)
                        packed[target_of(which, piece), at * HALF:(at + 1) * HALF] = block_b[
                            half * HALF:(half + 1) * HALF
                        ]
                        if r == c:
                            rest[(piece, at)] = jnp.sum(
                                jnp.where(eye, block - block_b.astype(F32), 0.0), axis=0, keepdims=True
                            )
        for piece in range(NZL * NY):
            lines = [rest.get((piece, at), jnp.zeros((1, TILE), F32)) for at in range(HALVES)]
            put_rest(packed.at[target_of(which, piece)], lines)
        for zl in range(NZL):
            part = pl.ds(target_of(which, zl * NY), NY)
            stores.append(
                pltpu.make_async_copy(packed.at[part], out_ref.at[part], out_sems.at[which, zl])
            )
            stores[-1].start()
    gradient_load.wait()
    y, own = lax.axis_index("y"), block_here()
    for shift, ref in enumerate(turn_refs):
        block = flip_scalar(jnp.bitwise_xor(own, lax.rem(y + shift, NY)))
        start = pl.multiple_of(block * ORDER, ORDER)
        ref[...] = gradient[0, :, pl.ds(start, ORDER)].astype(BF16)
    for store in stores:
        store.wait()


def target_of(which, piece):
    return (piece // NY * NXL + which) * NY + piece % NY


def put_rest(ref, lines):
    lines = lines + [jnp.zeros((1, TILE), F32)] * (REST - len(lines))
    ref[PIECE:PIECE + REST] = jnp.concatenate(lines, axis=0).astype(BF16)


def eye_of(piece, at):
    row = lax.broadcasted_iota(jnp.int32, (HALF, TILE), 0)
    return row + lax.rem(piece * HALVES + at, 2) * HALF == lax.broadcasted_iota(
        jnp.int32, (HALF, TILE), 1
    )


def sum_halves(piece, parts):
    def added(rows):
        return sum([part[rows].astype(F32) for part in parts[1:]], parts[0][rows].astype(F32))

    rest = added(slice(PIECE, PIECE + REST))
    halves = []
    for at in range(HALVES):
        total = added(slice(at * HALF, (at + 1) * HALF))
        halves.append(total + jnp.where(eye_of(piece, at), rest[at:at + 1], 0.0))
    return halves


def put_halves(piece, out_ref, halves, more=()):
    lines = []
    for at, half in enumerate(halves):
        half_b = half.astype(BF16)
        lines.append(
            jnp.sum(jnp.where(eye_of(piece, at), half - half_b.astype(F32), 0.0), axis=0, keepdims=True)
        )
        out_ref[at * HALF:(at + 1) * HALF] = half_b
    put_rest(out_ref, lines + list(more))


def sum_kernel(got_ref, *refs):
    turn_refs, (out_ref, slab_ref) = refs[:NY], refs[NY:]
    for turn, ref in enumerate(turn_refs):
        at = lax.rem(lax.axis_index("y") + NY - turn, NY) * ROWS
        slab_ref[pl.ds(pl.multiple_of(at, ROWS), ROWS), :] = ref[...]
    piece = piece_here()
    put_halves(piece, out_ref, sum_halves(piece, [got_ref.at[n] for n in range(got_ref.shape[0])]))


def damp_kernel(all_tokens, *refs):
    parts, (slab_ref, other_ref, out_ref, slabs_ref, damped, sems) = refs[:NZH], refs[NZH:]
    piece = piece_here()
    halves = []
    squares = jnp.zeros((HALF, TILE), F32)
    for at, half in enumerate(sum_halves(piece, parts)):
        block = lax.div(piece * HALVES + at, 2)
        on_diag = functools.reduce(jnp.logical_or, [block == WHERE[(r, r)] for r in range(GRID)])
        damping = jnp.where(on_diag, DAMPING, 0.0)
        half = half / all_tokens + jnp.where(eye_of(piece, at), damping, 0.0)
        squares = squares + jnp.where(on_diag, 1.0, 2.0) * half * half
        halves.append(half)
    left = jnp.sum(jnp.sum(squares, axis=0, keepdims=True), axis=1, keepdims=True)
    left = jnp.broadcast_to(left, (1, TILE))
    terms = []
    for _ in range(TERMS):
        terms.append(left.astype(BF16).astype(F32))
        left = left - terms[-1]
    put_halves(piece, damped, halves, terms)
    stores = [
        pltpu.make_async_copy(damped, out_ref.at[n], sems.at[n]) for n in range(out_ref.shape[0])
    ]
    for store in stores:
        store.start()
    zl, rows = lax.axis_index("zl"), NY * ROWS
    slabs_ref[pl.ds(pl.multiple_of(zl * rows, rows), rows), :] = slab_ref[...]
    slabs_ref[pl.ds(pl.multiple_of((1 - zl) * rows, rows), rows), :] = other_ref[...]
    for store in stores:
        store.wait()


def root_kernel(packed_ref, root_ref, scaled, iterate, iterate_b, square_b, cubic_b):
    terms = sum([packed_ref[n, PIECE:].astype(F32) for n in range(NZL * NY)])[HALVES:HALVES + TERMS]
    frob = jnp.sqrt(jnp.sum(terms, axis=0, keepdims=True)[:, 0:1])
    over_frob = 1.0 / frob
    over_root = 1.0 / jnp.sqrt(frob)
    for r, c in PAIRS:
        parts = []
        for half in range(2):
            piece, at = divmod(2 * WHERE[(r, c)] + half, HALVES)
            part = packed_ref[piece, at * HALF:(at + 1) * HALF].astype(F32)
            if r == c:
                rest = packed_ref[piece, PIECE:].astype(F32)[at:at + 1]
                part = part + jnp.where(eye_of(piece, at), rest, 0.0)
            parts.append(part)
        block = (jnp.concatenate(parts, axis=0) * over_frob).astype(BF16)
        scaled[r * TILE:(r + 1) * TILE, c * TILE:(c + 1) * TILE] = block
        if r != c:
            scaled[c * TILE:(c + 1) * TILE, r * TILE:(r + 1) * TILE] = block.T
    width = 2 * TILE
    tiles = [slice(n, n + width) for n in range(0, ORDER, width)]
    for s in tiles:
        row = lax.broadcasted_iota(jnp.int32, (ORDER, width), 0)
        col = lax.broadcasted_iota(jnp.int32, (ORDER, width), 1) + s.start
        first = 1.5 * (row == col).astype(F32) - 0.5 * scaled[:, s].astype(F32)
        iterate[:, s] = first
        iterate_b[:, s] = first.astype(BF16)
    for sweep in range(SWEEPS):
        for s in tiles:
            square_b[:, s] = jnp.dot(
                iterate_b[...], iterate_b[:, s], preferred_element_type=F32
            ).astype(BF16)
        for s in tiles:
            cubic_b[:, s] = jnp.dot(
                square_b[...], scaled[:, s], preferred_element_type=F32
            ).astype(BF16)
        for s in tiles:
            new = 1.5 * iterate[:, s] - 0.5 * jnp.dot(
                cubic_b[...], iterate_b[:, s], preferred_element_type=F32
            )
            if sweep < SWEEPS - 1:
                iterate[:, s] = new
            else:
                root_ref[:, s] = (new * over_root).astype(BF16)
        if sweep < SWEEPS - 1:
            for s in tiles:
                iterate_b[:, s] = iterate[:, s].astype(BF16)

def right_kernel(root_ref, *refs):
    slab_refs, right_refs, right = refs[:NXL], refs[NXL:NXL + NZH], refs[-1]
    zh, zl, rows = lax.axis_index("zh"), lax.axis_index("zl"), NY * ROWS
    cols = root_ref[:, pl.ds(pl.multiple_of(zl * (NZH * TILE), NZH * TILE), NZH * TILE)]
    for xl, ref in enumerate(slab_refs):
        done = jnp.dot(ref[...], cols, preferred_element_type=F32).astype(BF16)
        for n in range(NZL):
            right[(n * NXL + xl) * rows:(n * NXL + xl + 1) * rows] = done[n * rows:(n + 1) * rows]
    for shift, ref in zip(SHIFTS, right_refs):
        at = lax.rem(zh + shift, NZH) * TILE
        ref[...] = right[:, pl.ds(pl.multiple_of(at, TILE), TILE)]


def left_kernel(root_ref, *refs):
    right_refs, (out_ref, right) = refs[:NZH], refs[NZH:]
    for shift, ref in zip(SHIFTS, right_refs):
        at = lax.rem(lax.axis_index("zh") + NZH - shift, NZH) * ZROWS
        right[pl.ds(pl.multiple_of(at, ZROWS), ZROWS), :] = ref[...]
    out_ref[...] = jnp.dot(root_ref[...], right[...], preferred_element_type=F32).astype(BF16)


def place_kernel(got_ref, out_ref):
    own = block_here()
    for k in range(NBLOCK):
        y = jnp.bitwise_xor(own, flip(k))
        for z in range(NZ):
            at = k * ORDER + z % NZL * (NZH * TILE) + z // NZL * TILE
            out_ref[0, :, at:at + TILE] = got_ref[z * NXL * NY + y]


def place(xl, y, block):
    return (xl * NY + y) * NBLOCK + block


def turned(x, axes, size, shift):
    return lax.ppermute(x, axes, [(n, (n + shift) % size) for n in range(size)])


def local(acts, grads_out, gradient):
    all_tokens = acts.shape[0] * NZ * NXL * NY
    packed, *turns = call(
        gram_kernel,
        "gram",
        [jax.ShapeDtypeStruct((NZL * NXL * NY, PIECE + REST, TILE), BF16)]
        + [jax.ShapeDtypeStruct((ROWS, ORDER), BF16)] * NY,
        (acts, grads_out, gradient),
        specs=[HBM] * 3,
        out_specs=[HBM] + [VMEM] * NY,
        scratch=[
            pltpu.VMEM(acts.shape, BF16),
            pltpu.VMEM(acts.shape, BF16),
            pltpu.VMEM(gradient.shape, F32),
            pltpu.VMEM((NZL * NXL * NY, PIECE + REST, TILE), BF16),
            pltpu.SemaphoreType.DMA((2, LOADS)),
            pltpu.SemaphoreType.DMA(()),
            pltpu.SemaphoreType.DMA((2, NZL)),
        ],
        flops=4 * acts.shape[0] * ORDER * ORDER,
        vmem=60 << 20,
    )
    turns = [turns[0]] + [turned(turns[shift], "y", NY, shift) for shift in range(1, NY)]

    got = lax.all_to_all(packed, ("zl", "xl", "y"), 0, 0, tiled=True)
    part, slab = call(
        sum_kernel,
        "sum",
        [
            jax.ShapeDtypeStruct((PIECE + REST, TILE), BF16),
            jax.ShapeDtypeStruct((NY * ROWS, ORDER), BF16),
        ],
        (got, *turns),
    )
    other = turned(slab, "zl", NZL, 1)
    parts = [part] + [turned(part, "zh", NZH, shift) for shift in SHIFTS[2::-1]]
    pieces, slabs = call(
        functools.partial(damp_kernel, float(all_tokens)),
        "damp",
        [
            jax.ShapeDtypeStruct((NZL * NY, PIECE + REST, TILE), BF16),
            jax.ShapeDtypeStruct((NZL * NY * ROWS, ORDER), BF16),
        ],
        (*parts, slab, other),
        out_specs=[HBM, VMEM],
        scratch=[
            pltpu.VMEM((PIECE + REST, TILE), BF16),
            pltpu.SemaphoreType.DMA((NZL * NY,)),
        ],
    )
    cells = [(partner(k, y), k, y) for k in range(NBLOCK) for y in range(NY)]
    slabs = [
        lax.ppermute(
            slabs,
            ("xl", "y", "xh", "c"),
            [(place(xl, y, i), place(1, y, k)) for i, k, y in cells],
        )
        for xl in range(NXL)
    ]
    packed = lax.all_to_all(pieces, ("zl", "y"), 0, 0, tiled=True)

    square_b = pltpu.VMEM((ORDER, ORDER), BF16)
    right_done = jax.ShapeDtypeStruct((ZROWS, TILE), BF16)
    root = call(
        root_kernel,
        "root",
        jax.ShapeDtypeStruct((ORDER, ORDER), BF16),
        (packed,),
        scratch=[square_b, pltpu.VMEM((ORDER, ORDER), F32), square_b, square_b, square_b],
        flops=6 * SWEEPS * ORDER**3,
    )
    right_done = call(
        right_kernel,
        "right",
        [right_done] * NZH,
        (root, *slabs),
        scratch=[pltpu.VMEM((ZROWS, NZH * TILE), BF16)],
        flops=2 * ORDER * ZROWS * NZH * TILE,
    )

    count = NXL * NY * NBLOCK
    right_done = [
        lax.ppermute(
            right_done[n],
            ("zh", "xl", "y", "xh", "c"),
            [
                (zh * count + place(1, y, k), (zh + shift) % NZH * count + place(0, y, i))
                for zh in range(NZH)
                for i, k, y in cells
            ],
        )
        for n, shift in enumerate(SHIFTS)
    ]
    result = call(
        left_kernel,
        "left",
        jax.ShapeDtypeStruct((ORDER, TILE), BF16),
        (root, *right_done),
        scratch=[pltpu.VMEM((ORDER, TILE), BF16)],
        flops=2 * ORDER * ORDER * TILE,
    )
    result = result.reshape(NZ * NXL * NY, ROWS, TILE)
    returned = lax.all_to_all(result, DP, 0, 0, tiled=True)
    return call(
        place_kernel,
        "place",
        jax.ShapeDtypeStruct((1, ROWS, NBLOCK * ORDER), BF16),
        (returned,),
    )


def solution(mesh):
    split = Mesh(mesh.devices.reshape(SIZES), AXES)
    block = ("xh", "c")
    in_specs = (P(DP, block), P(DP, block), P(block, DP, None))
    out_specs = P(block, DP, None)
    return jax.shard_map(local, mesh=split, in_specs=in_specs, out_specs=out_specs, check_vma=False)
```

```python
import functools

import jax
import jax.numpy as jnp
from jax import lax
from jax.experimental import pallas as pl
from jax.experimental.pallas import tpu as pltpu
from jax.sharding import Mesh, PartitionSpec as P

F32, BF16 = jnp.float32, jnp.bfloat16
SWEEPS = 2
DAMPING = 0.05
TILE = 128
VMEM_BYTES = 48 << 20

AXES = ("zh", "zl", "xl", "y", "xh", "c")
SIZES = (4, 2, 2, 4, 2, 2)
NZH, NZL, NXL, NY, NXH, NC = SIZES
NZ, NBLOCK = NZH * NZL, NXH * NC
DP = ("zh", "zl", "xl", "y")

ORDER = 1024
GRID = ORDER // TILE
PAIRS = [(r, c) for r in range(GRID) for c in range(r, GRID)]
WHERE = {pair: n for n, pair in enumerate(PAIRS)}

HALF = TILE // 2
HALVES = 2 * len(PAIRS) // (NZL * NY)
PIECE = HALVES * HALF
REST = 16
ROWS = 16
TERMS = 3
SHIFTS = (2, 1, 3, 0)
LOADS = 4
ZROWS = NZL * NXL * NY * ROWS


def call(
    kernel, name, out_shape, args, specs=None, out_specs=None, scratch=(), flops=0, vmem=VMEM_BYTES
):
    extra = {} if specs is None else {"in_specs": specs}
    if out_specs is not None:
        extra["out_specs"] = out_specs
    return pl.pallas_call(
        kernel,
        out_shape=out_shape,
        scratch_shapes=list(scratch),
        compiler_params=pltpu.CompilerParams(vmem_limit_bytes=vmem),
        cost_estimate=pl.CostEstimate(flops=flops, bytes_accessed=4 << 20, transcendentals=0),
        name=name,
        **extra,
    )(*args)


HBM = pl.BlockSpec(memory_space=pltpu.HBM)
VMEM = pl.BlockSpec(memory_space=pltpu.VMEM)


def flip(block):
    return block // NC + block % NC * NXH


def partner(block, y):
    return flip(block) ^ y


def flip_scalar(block):
    return lax.div(block, NC) + lax.rem(block, NC) * NXH


def block_here():
    return lax.axis_index("xh") * NC + lax.axis_index("c")


def piece_here():
    return lax.axis_index("zl") * NY + lax.axis_index("y")


def gram_kernel(acts_ref, grads_ref, out_ref, acts, grads, packed, sems, out_sems):
    rows = acts.shape[0] // LOADS
    loads = []
    for which, (far, near) in enumerate(((acts_ref, acts), (grads_ref, grads))):
        for n in range(LOADS):
            part = pl.ds(n * rows, rows)
            loads.append(pltpu.make_async_copy(far.at[part], near.at[part], sems.at[which, n]))
            loads[-1].start()
    width = 2 * TILE
    eye = lax.broadcasted_iota(jnp.int32, (TILE, TILE), 0) == lax.broadcasted_iota(
        jnp.int32, (TILE, TILE), 1
    )
    stores = []
    for which, ref in enumerate((acts, grads)):
        for load in loads[which * LOADS:(which + 1) * LOADS]:
            load.wait()
        rest = {}
        for first in range(0, ORDER, width):
            slab = lax.dot_general(
                ref[:, first:first + width],
                ref[:, first:],
                (((0,), (0,)), ((), ())),
                preferred_element_type=F32,
            )
            for r in range(first // TILE, (first + width) // TILE):
                for c in range(r, GRID):
                    block = slab[
                        r * TILE - first:(r + 1) * TILE - first,
                        c * TILE - first:(c + 1) * TILE - first,
                    ]
                    block_b = block.astype(BF16)
                    for half in range(2):
                        piece, at = divmod(2 * WHERE[(r, c)] + half, HALVES)
                        packed[target_of(which, piece), at * HALF:(at + 1) * HALF] = block_b[
                            half * HALF:(half + 1) * HALF
                        ]
                        if r == c:
                            rest[(piece, at)] = jnp.sum(
                                jnp.where(eye, block - block_b.astype(F32), 0.0), axis=0, keepdims=True
                            )
        for piece in range(NZL * NY):
            lines = [rest.get((piece, at), jnp.zeros((1, TILE), F32)) for at in range(HALVES)]
            put_rest(packed.at[target_of(which, piece)], lines)
        for zl in range(NZL):
            part = pl.ds(target_of(which, zl * NY), NY)
            stores.append(
                pltpu.make_async_copy(packed.at[part], out_ref.at[part], out_sems.at[which, zl])
            )
            stores[-1].start()
    for store in stores:
        store.wait()


def target_of(which, piece):
    return (piece // NY * NXL + which) * NY + piece % NY


def put_rest(ref, lines):
    lines = lines + [jnp.zeros((1, TILE), F32)] * (REST - len(lines))
    ref[PIECE:PIECE + REST] = jnp.concatenate(lines, axis=0).astype(BF16)


def eye_of(piece, at):
    row = lax.broadcasted_iota(jnp.int32, (HALF, TILE), 0)
    return row + lax.rem(piece * HALVES + at, 2) * HALF == lax.broadcasted_iota(
        jnp.int32, (HALF, TILE), 1
    )


def sum_halves(piece, parts):
    def added(rows):
        return sum([part[rows].astype(F32) for part in parts[1:]], parts[0][rows].astype(F32))

    rest = added(slice(PIECE, PIECE + REST))
    halves = []
    for at in range(HALVES):
        total = added(slice(at * HALF, (at + 1) * HALF))
        halves.append(total + jnp.where(eye_of(piece, at), rest[at:at + 1], 0.0))
    return halves


def put_halves(piece, out_ref, halves, more=()):
    lines = []
    for at, half in enumerate(halves):
        half_b = half.astype(BF16)
        lines.append(
            jnp.sum(jnp.where(eye_of(piece, at), half - half_b.astype(F32), 0.0), axis=0, keepdims=True)
        )
        out_ref[at * HALF:(at + 1) * HALF] = half_b
    put_rest(out_ref, lines + list(more))


def sum_kernel(got_ref, gradient_ref, out_ref, *turn_refs):
    y, own = lax.axis_index("y"), block_here()
    for shift, ref in enumerate(turn_refs):
        block = flip_scalar(jnp.bitwise_xor(own, lax.rem(y + shift, NY)))
        start = pl.multiple_of(block * ORDER, ORDER)
        ref[...] = gradient_ref[0, :, pl.ds(start, ORDER)].astype(BF16)
    piece = piece_here()
    put_halves(piece, out_ref, sum_halves(piece, [got_ref.at[n] for n in range(got_ref.shape[0])]))


def damp_kernel(all_tokens, *refs):
    parts, turn_refs = refs[:NZH], refs[NZH:NZH + NY]
    out_ref, slab_ref, damped, sems = refs[NZH + NY:]
    piece = piece_here()
    halves = []
    squares = jnp.zeros((HALF, TILE), F32)
    for at, half in enumerate(sum_halves(piece, parts)):
        block = lax.div(piece * HALVES + at, 2)
        on_diag = functools.reduce(jnp.logical_or, [block == WHERE[(r, r)] for r in range(GRID)])
        damping = jnp.where(on_diag, DAMPING, 0.0)
        half = half / all_tokens + jnp.where(eye_of(piece, at), damping, 0.0)
        squares = squares + jnp.where(on_diag, 1.0, 2.0) * half * half
        halves.append(half)
    left = jnp.sum(jnp.sum(squares, axis=0, keepdims=True), axis=1, keepdims=True)
    left = jnp.broadcast_to(left, (1, TILE))
    terms = []
    for _ in range(TERMS):
        terms.append(left.astype(BF16).astype(F32))
        left = left - terms[-1]
    put_halves(piece, damped, halves, terms)
    stores = [
        pltpu.make_async_copy(damped, out_ref.at[n], sems.at[n]) for n in range(out_ref.shape[0])
    ]
    for store in stores:
        store.start()
    for turn, ref in enumerate(turn_refs):
        at = lax.rem(lax.axis_index("y") + NY - turn, NY) * ROWS
        slab_ref[pl.ds(pl.multiple_of(at, ROWS), ROWS), :] = ref[...]
    for store in stores:
        store.wait()


def root_kernel(packed_ref, root_ref, scaled, iterate, iterate_b, square_b, cubic_b):
    terms = sum([packed_ref[n, PIECE:].astype(F32) for n in range(NZL * NY)])[HALVES:HALVES + TERMS]
    frob = jnp.sqrt(jnp.sum(terms, axis=0, keepdims=True)[:, 0:1])
    over_frob = 1.0 / frob
    over_root = 1.0 / jnp.sqrt(frob)
    for r, c in PAIRS:
        parts = []
        for half in range(2):
            piece, at = divmod(2 * WHERE[(r, c)] + half, HALVES)
            part = packed_ref[piece, at * HALF:(at + 1) * HALF].astype(F32)
            if r == c:
                rest = packed_ref[piece, PIECE:].astype(F32)[at:at + 1]
                part = part + jnp.where(eye_of(piece, at), rest, 0.0)
            parts.append(part)
        block = (jnp.concatenate(parts, axis=0) * over_frob).astype(BF16)
        scaled[r * TILE:(r + 1) * TILE, c * TILE:(c + 1) * TILE] = block
        if r != c:
            scaled[c * TILE:(c + 1) * TILE, r * TILE:(r + 1) * TILE] = block.T
    width = 2 * TILE
    tiles = [slice(n, n + width) for n in range(0, ORDER, width)]
    for s in tiles:
        row = lax.broadcasted_iota(jnp.int32, (ORDER, width), 0)
        col = lax.broadcasted_iota(jnp.int32, (ORDER, width), 1) + s.start
        first = 1.5 * (row == col).astype(F32) - 0.5 * scaled[:, s].astype(F32)
        iterate[:, s] = first
        iterate_b[:, s] = first.astype(BF16)
    for sweep in range(SWEEPS):
        for s in tiles:
            square_b[:, s] = jnp.dot(
                iterate_b[...], iterate_b[:, s], preferred_element_type=F32
            ).astype(BF16)
        for s in tiles:
            cubic_b[:, s] = jnp.dot(
                square_b[...], scaled[:, s], preferred_element_type=F32
            ).astype(BF16)
        for s in tiles:
            new = 1.5 * iterate[:, s] - 0.5 * jnp.dot(
                cubic_b[...], iterate_b[:, s], preferred_element_type=F32
            )
            if sweep < SWEEPS - 1:
                iterate[:, s] = new
            else:
                root_ref[:, s] = (new * over_root).astype(BF16)
        if sweep < SWEEPS - 1:
            for s in tiles:
                iterate_b[:, s] = iterate[:, s].astype(BF16)

def right_kernel(root_ref, *refs):
    slab_refs, right_refs, right = refs[:NZL * NXL], refs[NZL * NXL:NZL * NXL + NZH], refs[-1]
    zh, zl, rows = lax.axis_index("zh"), lax.axis_index("zl"), NY * ROWS
    cols = root_ref[:, pl.ds(pl.multiple_of(zl * (NZH * TILE), NZH * TILE), NZH * TILE)]
    for turn, ref in enumerate(slab_refs):
        at = (lax.rem(zl + turn // NXL, NZL) * NXL + turn % NXL) * rows
        right[pl.ds(pl.multiple_of(at, rows), rows), :] = jnp.dot(
            ref[...], cols, preferred_element_type=F32
        ).astype(BF16)
    for shift, ref in zip(SHIFTS, right_refs):
        at = lax.rem(zh + shift, NZH) * TILE
        ref[...] = right[:, pl.ds(pl.multiple_of(at, TILE), TILE)]


def left_kernel(root_ref, *refs):
    right_refs, (out_ref, right) = refs[:NZH], refs[NZH:]
    for shift, ref in zip(SHIFTS, right_refs):
        at = lax.rem(lax.axis_index("zh") + NZH - shift, NZH) * ZROWS
        right[pl.ds(pl.multiple_of(at, ZROWS), ZROWS), :] = ref[...]
    out_ref[...] = jnp.dot(root_ref[...], right[...], preferred_element_type=F32).astype(BF16)


def place_kernel(got_ref, out_ref):
    own = block_here()
    for k in range(NBLOCK):
        y = jnp.bitwise_xor(own, flip(k))
        for z in range(NZ):
            at = k * ORDER + z % NZL * (NZH * TILE) + z // NZL * TILE
            out_ref[0, :, at:at + TILE] = got_ref[z * NXL * NY + y]


def place(xl, y, block):
    return (xl * NY + y) * NBLOCK + block


def turned(x, axes, size, shift):
    return lax.ppermute(x, axes, [(n, (n + shift) % size) for n in range(size)])


def local(acts, grads_out, gradient):
    all_tokens = acts.shape[0] * NZ * NXL * NY
    packed = call(
        gram_kernel,
        "gram",
        jax.ShapeDtypeStruct((NZL * NXL * NY, PIECE + REST, TILE), BF16),
        (acts, grads_out),
        specs=[HBM] * 2,
        out_specs=HBM,
        scratch=[
            pltpu.VMEM(acts.shape, BF16),
            pltpu.VMEM(acts.shape, BF16),
            pltpu.VMEM((NZL * NXL * NY, PIECE + REST, TILE), BF16),
            pltpu.SemaphoreType.DMA((2, LOADS)),
            pltpu.SemaphoreType.DMA((2, NZL)),
        ],
        flops=4 * acts.shape[0] * ORDER * ORDER,
        vmem=60 << 20,
    )

    got = lax.all_to_all(packed, ("zl", "xl", "y"), 0, 0, tiled=True)
    part, *turns = call(
        sum_kernel,
        "sum",
        [jax.ShapeDtypeStruct((PIECE + REST, TILE), BF16)]
        + [jax.ShapeDtypeStruct((ROWS, ORDER), BF16)] * NY,
        (got, gradient),
    )
    turns = [turns[0]] + [turned(turns[shift], "y", NY, shift) for shift in range(1, NY)]
    parts = [part] + [turned(part, "zh", NZH, shift) for shift in SHIFTS[2::-1]]
    pieces, slab = call(
        functools.partial(damp_kernel, float(all_tokens)),
        "damp",
        [
            jax.ShapeDtypeStruct((NZL * NY, PIECE + REST, TILE), BF16),
            jax.ShapeDtypeStruct((NY * ROWS, ORDER), BF16),
        ],
        (*parts, *turns),
        out_specs=[HBM, VMEM],
        scratch=[
            pltpu.VMEM((PIECE + REST, TILE), BF16),
            pltpu.SemaphoreType.DMA((NZL * NY,)),
        ],
    )
    count = NXL * NY * NBLOCK
    cells = [(partner(k, y), k, y) for k in range(NBLOCK) for y in range(NY)]
    slabs = [
        lax.ppermute(
            slab,
            ("zl", "xl", "y", "xh", "c"),
            [
                ((zl + turn) % NZL * count + place(xl, y, i), zl * count + place(1, y, k))
                for zl in range(NZL)
                for i, k, y in cells
            ],
        )
        for turn in range(NZL)
        for xl in range(NXL)
    ]
    packed = lax.all_to_all(pieces, ("zl", "y"), 0, 0, tiled=True)

    square_b = pltpu.VMEM((ORDER, ORDER), BF16)
    right_done = jax.ShapeDtypeStruct((ZROWS, TILE), BF16)
    root = call(
        root_kernel,
        "root",
        jax.ShapeDtypeStruct((ORDER, ORDER), BF16),
        (packed,),
        scratch=[square_b, pltpu.VMEM((ORDER, ORDER), F32), square_b, square_b, square_b],
        flops=6 * SWEEPS * ORDER**3,
    )
    right_done = call(
        right_kernel,
        "right",
        [right_done] * NZH,
        (root, *slabs),
        scratch=[pltpu.VMEM((ZROWS, NZH * TILE), BF16)],
        flops=2 * ORDER * ZROWS * NZH * TILE,
    )

    right_done = [
        lax.ppermute(
            right_done[n],
            ("zh", "xl", "y", "xh", "c"),
            [
                (zh * count + place(1, y, k), (zh + shift) % NZH * count + place(0, y, i))
                for zh in range(NZH)
                for i, k, y in cells
            ],
        )
        for n, shift in enumerate(SHIFTS)
    ]
    result = call(
        left_kernel,
        "left",
        jax.ShapeDtypeStruct((ORDER, TILE), BF16),
        (root, *right_done),
        scratch=[pltpu.VMEM((ORDER, TILE), BF16)],
        flops=2 * ORDER * ORDER * TILE,
    )
    result = result.reshape(NZ * NXL * NY, ROWS, TILE)
    returned = lax.all_to_all(result, DP, 0, 0, tiled=True)
    return call(
        place_kernel,
        "place",
        jax.ShapeDtypeStruct((1, ROWS, NBLOCK * ORDER), BF16),
        (returned,),
    )


def solution(mesh):
    split = Mesh(mesh.devices.reshape(SIZES), AXES)
    block = ("xh", "c")
    in_specs = (P(DP, block), P(DP, block), P(block, DP, None))
    out_specs = P(block, DP, None)
    return jax.shard_map(local, mesh=split, in_specs=in_specs, out_specs=out_specs, check_vma=False)
```

```python
import functools

import jax
import jax.numpy as jnp
from jax import lax
from jax.experimental import pallas as pl
from jax.experimental.pallas import tpu as pltpu
from jax.sharding import Mesh, PartitionSpec as P

F32, BF16 = jnp.float32, jnp.bfloat16
SWEEPS = 2
DAMPING = 0.05
TILE = 128
VMEM_BYTES = 28 << 20

AXES = ("zh", "zl", "xl", "y", "xh", "c")
SIZES = (4, 2, 2, 4, 2, 2)
NZH, NZL, NXL, NY, NXH, NC = SIZES
NZ, NBLOCK = NZH * NZL, NXH * NC
DP = ("zh", "zl", "xl", "y")

ORDER = 1024
GRID = ORDER // TILE
PAIRS = [(r, c) for r in range(GRID) for c in range(r, GRID)]
WHERE = {pair: n for n, pair in enumerate(PAIRS)}

HALF = TILE // 2
HALVES = 2 * len(PAIRS) // (NZL * NY)
PIECE = HALVES * HALF
REST = 16
ROWS = 16
TERMS = 3
SHIFTS = (2, 1, 3, 0)
LOADS = 4
ZROWS = NZL * NXL * NY * ROWS


def call(
    kernel, name, out_shape, args, specs=None, out_specs=None, scratch=(), flops=0, vmem=VMEM_BYTES
):
    extra = {} if specs is None else {"in_specs": specs}
    if out_specs is not None:
        extra["out_specs"] = out_specs
    return pl.pallas_call(
        kernel,
        out_shape=out_shape,
        scratch_shapes=list(scratch),
        compiler_params=pltpu.CompilerParams(vmem_limit_bytes=vmem),
        cost_estimate=pl.CostEstimate(flops=flops, bytes_accessed=4 << 20, transcendentals=0),
        name=name,
        **extra,
    )(*args)


HBM = pl.BlockSpec(memory_space=pltpu.HBM)
VMEM = pl.BlockSpec(memory_space=pltpu.VMEM)


def flip(block):
    return block // NC + block % NC * NXH


def partner(block, y):
    return flip(block) ^ y


def flip_scalar(block):
    return lax.div(block, NC) + lax.rem(block, NC) * NXH


def block_here():
    return lax.axis_index("xh") * NC + lax.axis_index("c")


def piece_here():
    return lax.axis_index("zl") * NY + lax.axis_index("y")


def gram_kernel(acts_ref, grads_ref, out_ref, acts, grads, packed, sems, out_sems):
    rows = acts.shape[0] // LOADS
    loads = []
    for which, (far, near) in enumerate(((acts_ref, acts), (grads_ref, grads))):
        for n in range(LOADS):
            part = pl.ds(n * rows, rows)
            loads.append(pltpu.make_async_copy(far.at[part], near.at[part], sems.at[which, n]))
            loads[-1].start()
    width = 2 * TILE
    eye = lax.broadcasted_iota(jnp.int32, (TILE, TILE), 0) == lax.broadcasted_iota(
        jnp.int32, (TILE, TILE), 1
    )
    stores = []
    for which, ref in enumerate((acts, grads)):
        for load in loads[which * LOADS:(which + 1) * LOADS]:
            load.wait()
        rest = {}
        for first in range(0, ORDER, width):
            slab = lax.dot_general(
                ref[:, first:first + width],
                ref[:, first:],
                (((0,), (0,)), ((), ())),
                preferred_element_type=F32,
            )
            for r in range(first // TILE, (first + width) // TILE):
                for c in range(r, GRID):
                    block = slab[
                        r * TILE - first:(r + 1) * TILE - first,
                        c * TILE - first:(c + 1) * TILE - first,
                    ]
                    block_b = block.astype(BF16)
                    for half in range(2):
                        piece, at = divmod(2 * WHERE[(r, c)] + half, HALVES)
                        packed[target_of(which, piece), at * HALF:(at + 1) * HALF] = block_b[
                            half * HALF:(half + 1) * HALF
                        ]
                        if r == c:
                            rest[(piece, at)] = jnp.sum(
                                jnp.where(eye, block - block_b.astype(F32), 0.0), axis=0, keepdims=True
                            )
        for piece in range(NZL * NY):
            lines = [rest.get((piece, at), jnp.zeros((1, TILE), F32)) for at in range(HALVES)]
            put_rest(packed.at[target_of(which, piece)], lines)
        for zl in range(NZL):
            part = pl.ds(target_of(which, zl * NY), NY)
            stores.append(
                pltpu.make_async_copy(packed.at[part], out_ref.at[part], out_sems.at[which, zl])
            )
            stores[-1].start()
    for store in stores:
        store.wait()


def target_of(which, piece):
    return (piece // NY * NXL + which) * NY + piece % NY


def put_rest(ref, lines):
    lines = lines + [jnp.zeros((1, TILE), F32)] * (REST - len(lines))
    ref[PIECE:PIECE + REST] = jnp.concatenate(lines, axis=0).astype(BF16)


def eye_of(piece, at):
    row = lax.broadcasted_iota(jnp.int32, (HALF, TILE), 0)
    return row + lax.rem(piece * HALVES + at, 2) * HALF == lax.broadcasted_iota(
        jnp.int32, (HALF, TILE), 1
    )


def sum_halves(piece, parts):
    def added(rows):
        return sum([part[rows].astype(F32) for part in parts[1:]], parts[0][rows].astype(F32))

    rest = added(slice(PIECE, PIECE + REST))
    halves = []
    for at in range(HALVES):
        total = added(slice(at * HALF, (at + 1) * HALF))
        halves.append(total + jnp.where(eye_of(piece, at), rest[at:at + 1], 0.0))
    return halves


def put_halves(piece, out_ref, halves, more=()):
    lines = []
    for at, half in enumerate(halves):
        half_b = half.astype(BF16)
        lines.append(
            jnp.sum(jnp.where(eye_of(piece, at), half - half_b.astype(F32), 0.0), axis=0, keepdims=True)
        )
        out_ref[at * HALF:(at + 1) * HALF] = half_b
    put_rest(out_ref, lines + list(more))


def sum_kernel(got_ref, gradient_ref, out_ref, *turn_refs):
    y, own = lax.axis_index("y"), block_here()
    for shift, ref in enumerate(turn_refs):
        block = flip_scalar(jnp.bitwise_xor(own, lax.rem(y + shift, NY)))
        start = pl.multiple_of(block * ORDER, ORDER)
        ref[...] = gradient_ref[0, :, pl.ds(start, ORDER)].astype(BF16)
    piece = piece_here()
    put_halves(piece, out_ref, sum_halves(piece, [got_ref.at[n] for n in range(got_ref.shape[0])]))


def damp_kernel(all_tokens, *refs):
    parts, turn_refs = refs[:NZH], refs[NZH:NZH + NY]
    out_ref, slab_ref, damped, sems = refs[NZH + NY:]
    piece = piece_here()
    halves = []
    squares = jnp.zeros((HALF, TILE), F32)
    for at, half in enumerate(sum_halves(piece, parts)):
        block = lax.div(piece * HALVES + at, 2)
        on_diag = functools.reduce(jnp.logical_or, [block == WHERE[(r, r)] for r in range(GRID)])
        damping = jnp.where(on_diag, DAMPING, 0.0)
        half = half / all_tokens + jnp.where(eye_of(piece, at), damping, 0.0)
        squares = squares + jnp.where(on_diag, 1.0, 2.0) * half * half
        halves.append(half)
    left = jnp.sum(jnp.sum(squares, axis=0, keepdims=True), axis=1, keepdims=True)
    left = jnp.broadcast_to(left, (1, TILE))
    terms = []
    for _ in range(TERMS):
        terms.append(left.astype(BF16).astype(F32))
        left = left - terms[-1]
    put_halves(piece, damped, halves, terms)
    stores = [
        pltpu.make_async_copy(damped, out_ref.at[n], sems.at[n]) for n in range(out_ref.shape[0])
    ]
    for store in stores:
        store.start()
    for turn, ref in enumerate(turn_refs):
        at = lax.rem(lax.axis_index("y") + NY - turn, NY) * ROWS
        slab_ref[pl.ds(pl.multiple_of(at, ROWS), ROWS), :] = ref[...]
    for store in stores:
        store.wait()


def root_kernel(packed_ref, over_ref, iterate, iterate_b, cubic_b, scaled, square_b):
    terms = sum([packed_ref[n, PIECE:].astype(F32) for n in range(NZL * NY)])[HALVES:HALVES + TERMS]
    frob = jnp.sqrt(jnp.sum(terms, axis=0, keepdims=True)[:, 0:1])
    over_frob = 1.0 / frob
    over_ref[...] = jnp.broadcast_to(1.0 / jnp.sqrt(frob), over_ref.shape)
    for r, c in PAIRS:
        parts = []
        for half in range(2):
            piece, at = divmod(2 * WHERE[(r, c)] + half, HALVES)
            part = packed_ref[piece, at * HALF:(at + 1) * HALF].astype(F32)
            if r == c:
                rest = packed_ref[piece, PIECE:].astype(F32)[at:at + 1]
                part = part + jnp.where(eye_of(piece, at), rest, 0.0)
            parts.append(part)
        block = (jnp.concatenate(parts, axis=0) * over_frob).astype(BF16)
        scaled[r * TILE:(r + 1) * TILE, c * TILE:(c + 1) * TILE] = block
        if r != c:
            scaled[c * TILE:(c + 1) * TILE, r * TILE:(r + 1) * TILE] = block.T
    width = 2 * TILE
    tiles = [slice(n, n + width) for n in range(0, ORDER, width)]
    for s in tiles:
        row = lax.broadcasted_iota(jnp.int32, (ORDER, width), 0)
        col = lax.broadcasted_iota(jnp.int32, (ORDER, width), 1) + s.start
        first = 1.5 * (row == col).astype(F32) - 0.5 * scaled[:, s].astype(F32)
        iterate[:, s] = first
        iterate_b[:, s] = first.astype(BF16)
    for sweep in range(SWEEPS):
        for s in tiles:
            upper = jnp.dot(
                iterate_b[:s.stop], iterate_b[:, s], preferred_element_type=F32
            ).astype(BF16)
            square_b[:s.stop, s] = upper
            for t in tiles[:s.start // width]:
                square_b[s, t] = upper[t].T
        for s in tiles:
            cubic_b[:, s] = jnp.dot(
                square_b[...], scaled[:, s], preferred_element_type=F32
            ).astype(BF16)
        if sweep < SWEEPS - 1:
            for s in tiles:
                iterate[:, s] = last_product(iterate[:, s], cubic_b, iterate_b[:, s])
            for s in tiles:
                iterate_b[:, s] = iterate[:, s].astype(BF16)


def last_product(iterate, cubic_b, iterate_b):
    return 1.5 * iterate - 0.5 * jnp.dot(cubic_b[...], iterate_b, preferred_element_type=F32)


def rest_kernel(over_ref, iterate, iterate_b, cubic_b, root_ref):
    width = 2 * TILE
    for s in [slice(n, n + width) for n in range(0, ORDER, width)]:
        new = last_product(iterate[:, s], cubic_b, iterate_b[:, s])
        root_ref[:, s] = (new * over_ref[0:1, 0:1]).astype(BF16)


def right_kernel(over_ref, iterate, iterate_b, cubic_b, *refs):
    slab_refs, right_refs, right = refs[:NZL * NXL], refs[NZL * NXL:NZL * NXL + NZH], refs[-1]
    zh, zl, rows = lax.axis_index("zh"), lax.axis_index("zl"), NY * ROWS
    here = pl.ds(pl.multiple_of(zl * (NZH * TILE), NZH * TILE), NZH * TILE)
    cols = last_product(iterate[:, here], cubic_b, iterate_b[:, here])
    cols = (cols * over_ref[0:1, 0:1]).astype(BF16)
    for turn, ref in enumerate(slab_refs):
        at = (lax.rem(zl + turn // NXL, NZL) * NXL + turn % NXL) * rows
        right[pl.ds(pl.multiple_of(at, rows), rows), :] = jnp.dot(
            ref[...], cols, preferred_element_type=F32
        ).astype(BF16)
    for shift, ref in zip(SHIFTS, right_refs):
        at = lax.rem(zh + shift, NZH) * TILE
        ref[...] = right[:, pl.ds(pl.multiple_of(at, TILE), TILE)]


def left_kernel(root_ref, *refs):
    right_refs, (out_ref, right) = refs[:NZH], refs[NZH:]
    for shift, ref in zip(SHIFTS, right_refs):
        at = lax.rem(lax.axis_index("zh") + NZH - shift, NZH) * ZROWS
        right[pl.ds(pl.multiple_of(at, ZROWS), ZROWS), :] = ref[...]
    out_ref[...] = jnp.dot(root_ref[...], right[...], preferred_element_type=F32).astype(BF16)


def place_kernel(got_ref, out_ref):
    own = block_here()
    for k in range(NBLOCK):
        y = jnp.bitwise_xor(own, flip(k))
        for z in range(NZ):
            at = k * ORDER + z % NZL * (NZH * TILE) + z // NZL * TILE
            out_ref[0, :, at:at + TILE] = got_ref[z * NXL * NY + y]


def place(xl, y, block):
    return (xl * NY + y) * NBLOCK + block


def turned(x, axes, size, shift):
    return lax.ppermute(x, axes, [(n, (n + shift) % size) for n in range(size)])


def local(acts, grads_out, gradient):
    all_tokens = acts.shape[0] * NZ * NXL * NY
    packed = call(
        gram_kernel,
        "gram",
        jax.ShapeDtypeStruct((NZL * NXL * NY, PIECE + REST, TILE), BF16),
        (acts, grads_out),
        specs=[HBM] * 2,
        out_specs=HBM,
        scratch=[
            pltpu.VMEM(acts.shape, BF16),
            pltpu.VMEM(acts.shape, BF16),
            pltpu.VMEM((NZL * NXL * NY, PIECE + REST, TILE), BF16),
            pltpu.SemaphoreType.DMA((2, LOADS)),
            pltpu.SemaphoreType.DMA((2, NZL)),
        ],
        flops=4 * acts.shape[0] * ORDER * ORDER,
        vmem=60 << 20,
    )

    got = lax.all_to_all(packed, ("zl", "xl", "y"), 0, 0, tiled=True)
    part, *turns = call(
        sum_kernel,
        "sum",
        [jax.ShapeDtypeStruct((PIECE + REST, TILE), BF16)]
        + [jax.ShapeDtypeStruct((ROWS, ORDER), BF16)] * NY,
        (got, gradient),
    )
    turns = [turns[0]] + [turned(turns[shift], "y", NY, shift) for shift in range(1, NY)]
    parts = [part] + [turned(part, "zh", NZH, shift) for shift in SHIFTS[2::-1]]
    pieces, slab = call(
        functools.partial(damp_kernel, float(all_tokens)),
        "damp",
        [
            jax.ShapeDtypeStruct((NZL * NY, PIECE + REST, TILE), BF16),
            jax.ShapeDtypeStruct((NY * ROWS, ORDER), BF16),
        ],
        (*parts, *turns),
        out_specs=[HBM, VMEM],
        scratch=[
            pltpu.VMEM((PIECE + REST, TILE), BF16),
            pltpu.SemaphoreType.DMA((NZL * NY,)),
        ],
    )
    count = NXL * NY * NBLOCK
    cells = [(partner(k, y), k, y) for k in range(NBLOCK) for y in range(NY)]
    slabs = [
        lax.ppermute(
            slab,
            ("zl", "xl", "y", "xh", "c"),
            [
                ((zl + turn) % NZL * count + place(xl, y, i), zl * count + place(1, y, k))
                for zl in range(NZL)
                for i, k, y in cells
            ],
        )
        for turn in range(NZL)
        for xl in range(NXL)
    ]
    packed = lax.all_to_all(pieces, ("zl", "y"), 0, 0, tiled=True)

    square_b = pltpu.VMEM((ORDER, ORDER), BF16)
    right_done = jax.ShapeDtypeStruct((ZROWS, TILE), BF16)
    square = jax.ShapeDtypeStruct((ORDER, ORDER), BF16)
    factors = call(
        root_kernel,
        "root",
        [
            jax.ShapeDtypeStruct((8, TILE), F32),
            jax.ShapeDtypeStruct((ORDER, ORDER), F32),
            square,
            square,
        ],
        (packed,),
        scratch=[square_b, square_b],
        flops=10 * ORDER**3,
    )
    right_done = call(
        right_kernel,
        "right",
        [right_done] * NZH,
        (*factors, *slabs),
        scratch=[pltpu.VMEM((ZROWS, NZH * TILE), BF16)],
        flops=2 * ORDER * (ZROWS + ORDER) * NZH * TILE,
    )
    root = call(rest_kernel, "rest", square, factors, flops=2 * ORDER**3)

    right_done = [
        lax.ppermute(
            right_done[n],
            ("zh", "xl", "y", "xh", "c"),
            [
                (zh * count + place(1, y, k), (zh + shift) % NZH * count + place(0, y, i))
                for zh in range(NZH)
                for i, k, y in cells
            ],
        )
        for n, shift in enumerate(SHIFTS)
    ]
    result = call(
        left_kernel,
        "left",
        jax.ShapeDtypeStruct((ORDER, TILE), BF16),
        (root, *right_done),
        scratch=[pltpu.VMEM((ORDER, TILE), BF16)],
        flops=2 * ORDER * ORDER * TILE,
    )
    result = result.reshape(NZ * NXL * NY, ROWS, TILE)
    returned = lax.all_to_all(result, DP, 0, 0, tiled=True)
    return call(
        place_kernel,
        "place",
        jax.ShapeDtypeStruct((1, ROWS, NBLOCK * ORDER), BF16),
        (returned,),
    )


def solution(mesh):
    split = Mesh(mesh.devices.reshape(SIZES), AXES)
    block = ("xh", "c")
    in_specs = (P(DP, block), P(DP, block), P(block, DP, None))
    out_specs = P(block, DP, None)
    return jax.shard_map(local, mesh=split, in_specs=in_specs, out_specs=out_specs, check_vma=False)
```

```python
import functools

import jax
import jax.numpy as jnp
from jax import lax
from jax.experimental import pallas as pl
from jax.experimental.pallas import tpu as pltpu
from jax.sharding import Mesh, PartitionSpec as P

F32, BF16 = jnp.float32, jnp.bfloat16
SWEEPS = 2
DAMPING = 0.05
TILE = 128
VMEM_BYTES = 28 << 20

AXES = ("zh", "zl", "xl", "y", "xh", "c")
SIZES = (4, 2, 2, 4, 2, 2)
NZH, NZL, NXL, NY, NXH, NC = SIZES
NZ, NBLOCK = NZH * NZL, NXH * NC
DP = ("zh", "zl", "xl", "y")

ORDER = 1024
GRID = ORDER // TILE
PAIRS = [(r, c) for r in range(GRID) for c in range(r, GRID)]
WHERE = {pair: n for n, pair in enumerate(PAIRS)}

HALF = TILE // 2
HALVES = 2 * len(PAIRS) // (NZL * NY)
PIECE = HALVES * HALF
REST = 16
ROWS = 16
TERMS = 3
SHIFTS = (2, 1, 3, 0)
LOADS = 4
ZROWS = NZL * NXL * NY * ROWS


def call(
    kernel, name, out_shape, args, specs=None, out_specs=None, scratch=(), flops=0, vmem=VMEM_BYTES
):
    extra = {} if specs is None else {"in_specs": specs}
    if out_specs is not None:
        extra["out_specs"] = out_specs
    return pl.pallas_call(
        kernel,
        out_shape=out_shape,
        scratch_shapes=list(scratch),
        compiler_params=pltpu.CompilerParams(vmem_limit_bytes=vmem),
        cost_estimate=pl.CostEstimate(flops=flops, bytes_accessed=4 << 20, transcendentals=0),
        name=name,
        **extra,
    )(*args)


HBM = pl.BlockSpec(memory_space=pltpu.HBM)
VMEM = pl.BlockSpec(memory_space=pltpu.VMEM)


def flip(block):
    return block // NC + block % NC * NXH


def partner(block, y):
    return flip(block) ^ y


def flip_scalar(block):
    return lax.div(block, NC) + lax.rem(block, NC) * NXH


def block_here():
    return lax.axis_index("xh") * NC + lax.axis_index("c")


def piece_here():
    return lax.axis_index("zl") * NY + lax.axis_index("y")


def gram_kernel(acts_ref, grads_ref, out_ref, acts, grads, packed, sems, out_sems):
    rows = acts.shape[0] // LOADS
    loads = []
    for which, (far, near) in enumerate(((acts_ref, acts), (grads_ref, grads))):
        for n in range(LOADS):
            part = pl.ds(n * rows, rows)
            loads.append(pltpu.make_async_copy(far.at[part], near.at[part], sems.at[which, n]))
            loads[-1].start()
    width = 2 * TILE
    eye = lax.broadcasted_iota(jnp.int32, (TILE, TILE), 0) == lax.broadcasted_iota(
        jnp.int32, (TILE, TILE), 1
    )
    stores = []
    for which, ref in enumerate((acts, grads)):
        for load in loads[which * LOADS:(which + 1) * LOADS]:
            load.wait()
        rest = {}
        for first in range(0, ORDER, width):
            slab = lax.dot_general(
                ref[:, first:first + width],
                ref[:, first:],
                (((0,), (0,)), ((), ())),
                preferred_element_type=F32,
            )
            for r in range(first // TILE, (first + width) // TILE):
                for c in range(r, GRID):
                    block = slab[
                        r * TILE - first:(r + 1) * TILE - first,
                        c * TILE - first:(c + 1) * TILE - first,
                    ]
                    block_b = block.astype(BF16)
                    for half in range(2):
                        piece, at = divmod(2 * WHERE[(r, c)] + half, HALVES)
                        packed[target_of(which, piece), at * HALF:(at + 1) * HALF] = block_b[
                            half * HALF:(half + 1) * HALF
                        ]
                        if r == c:
                            rest[(piece, at)] = jnp.sum(
                                jnp.where(eye, block - block_b.astype(F32), 0.0), axis=0, keepdims=True
                            )
            last = 2 * WHERE[(first // TILE + 1, GRID - 1)] + 2
            for piece in range(len(stores) - which * NZL * NY, last // HALVES):
                lines = [rest.get((piece, at), jnp.zeros((1, TILE), F32)) for at in range(HALVES)]
                target = target_of(which, piece)
                put_rest(packed.at[target], lines)
                stores.append(
                    pltpu.make_async_copy(
                        packed.at[target], out_ref.at[target], out_sems.at[which, piece]
                    )
                )
                stores[-1].start()
    for store in stores:
        store.wait()


def target_of(which, piece):
    return (piece // NY * NXL + which) * NY + piece % NY


def put_rest(ref, lines):
    lines = lines + [jnp.zeros((1, TILE), F32)] * (REST - len(lines))
    ref[PIECE:PIECE + REST] = jnp.concatenate(lines, axis=0).astype(BF16)


def eye_of(piece, at):
    row = lax.broadcasted_iota(jnp.int32, (HALF, TILE), 0)
    return row + lax.rem(piece * HALVES + at, 2) * HALF == lax.broadcasted_iota(
        jnp.int32, (HALF, TILE), 1
    )


def sum_halves(piece, parts):
    def added(rows):
        return sum([part[rows].astype(F32) for part in parts[1:]], parts[0][rows].astype(F32))

    rest = added(slice(PIECE, PIECE + REST))
    halves = []
    for at in range(HALVES):
        total = added(slice(at * HALF, (at + 1) * HALF))
        halves.append(total + jnp.where(eye_of(piece, at), rest[at:at + 1], 0.0))
    return halves


def put_halves(piece, out_ref, halves, more=()):
    lines = []
    for at, half in enumerate(halves):
        half_b = half.astype(BF16)
        lines.append(
            jnp.sum(jnp.where(eye_of(piece, at), half - half_b.astype(F32), 0.0), axis=0, keepdims=True)
        )
        out_ref[at * HALF:(at + 1) * HALF] = half_b
    put_rest(out_ref, lines + list(more))


def sum_kernel(got_ref, gradient_ref, out_ref, *turn_refs):
    y, own = lax.axis_index("y"), block_here()
    for shift, ref in enumerate(turn_refs):
        block = flip_scalar(jnp.bitwise_xor(own, lax.rem(y + shift, NY)))
        start = pl.multiple_of(block * ORDER, ORDER)
        ref[...] = gradient_ref[0, :, pl.ds(start, ORDER)].astype(BF16)
    piece = piece_here()
    put_halves(piece, out_ref, sum_halves(piece, [got_ref.at[n] for n in range(got_ref.shape[0])]))


def damp_kernel(all_tokens, *refs):
    parts, (out_ref, done_ref, damped, sems) = refs[:NZH], refs[NZH:]
    piece = piece_here()
    halves = []
    squares = jnp.zeros((HALF, TILE), F32)
    for at, half in enumerate(sum_halves(piece, parts)):
        block = lax.div(piece * HALVES + at, 2)
        on_diag = functools.reduce(jnp.logical_or, [block == WHERE[(r, r)] for r in range(GRID)])
        damping = jnp.where(on_diag, DAMPING, 0.0)
        half = half / all_tokens + jnp.where(eye_of(piece, at), damping, 0.0)
        squares = squares + jnp.where(on_diag, 1.0, 2.0) * half * half
        halves.append(half)
    left = jnp.sum(jnp.sum(squares, axis=0, keepdims=True), axis=1, keepdims=True)
    left = jnp.broadcast_to(left, (1, TILE))
    terms = []
    for _ in range(TERMS):
        terms.append(left.astype(BF16).astype(F32))
        left = left - terms[-1]
    put_halves(piece, damped, halves, terms)
    stores = [
        pltpu.make_async_copy(damped, out_ref.at[n], sems.at[n]) for n in range(out_ref.shape[0])
    ]
    for store in stores:
        store.start()
    done_ref[...] = jnp.zeros(done_ref.shape, F32)
    for store in stores:
        store.wait()


def join_kernel(done_ref, *refs):
    turn_refs, slab_ref = refs[:NY], refs[NY]
    for turn, ref in enumerate(turn_refs):
        at = lax.rem(lax.axis_index("y") + NY - turn, NY) * ROWS
        slab_ref[pl.ds(pl.multiple_of(at, ROWS), ROWS), :] = ref[...]


def root_kernel(packed_ref, over_ref, iterate, iterate_b, cubic_b, scaled, square_b):
    terms = sum([packed_ref[n, PIECE:].astype(F32) for n in range(NZL * NY)])[HALVES:HALVES + TERMS]
    frob = jnp.sqrt(jnp.sum(terms, axis=0, keepdims=True)[:, 0:1])
    over_frob = 1.0 / frob
    over_ref[...] = jnp.broadcast_to(1.0 / jnp.sqrt(frob), over_ref.shape)
    for r, c in PAIRS:
        parts = []
        for half in range(2):
            piece, at = divmod(2 * WHERE[(r, c)] + half, HALVES)
            part = packed_ref[piece, at * HALF:(at + 1) * HALF].astype(F32)
            if r == c:
                rest = packed_ref[piece, PIECE:].astype(F32)[at:at + 1]
                part = part + jnp.where(eye_of(piece, at), rest, 0.0)
            parts.append(part)
        block = (jnp.concatenate(parts, axis=0) * over_frob).astype(BF16)
        scaled[r * TILE:(r + 1) * TILE, c * TILE:(c + 1) * TILE] = block
        if r != c:
            scaled[c * TILE:(c + 1) * TILE, r * TILE:(r + 1) * TILE] = block.T
    width = 2 * TILE
    tiles = [slice(n, n + width) for n in range(0, ORDER, width)]
    for s in tiles:
        row = lax.broadcasted_iota(jnp.int32, (ORDER, width), 0)
        col = lax.broadcasted_iota(jnp.int32, (ORDER, width), 1) + s.start
        first = 1.5 * (row == col).astype(F32) - 0.5 * scaled[:, s].astype(F32)
        iterate[:, s] = first
        iterate_b[:, s] = first.astype(BF16)
    for sweep in range(SWEEPS):
        for s in tiles:
            upper = jnp.dot(
                iterate_b[:s.stop], iterate_b[:, s], preferred_element_type=F32
            ).astype(BF16)
            square_b[:s.stop, s] = upper
            for t in tiles[:s.start // width]:
                square_b[s, t] = upper[t].T
        for s in tiles:
            cubic_b[:, s] = jnp.dot(
                square_b[...], scaled[:, s], preferred_element_type=F32
            ).astype(BF16)
        if sweep < SWEEPS - 1:
            for s in tiles:
                iterate[:, s] = last_product(iterate[:, s], cubic_b, iterate_b[:, s])
            for s in tiles:
                iterate_b[:, s] = iterate[:, s].astype(BF16)


def last_product(iterate, cubic_b, iterate_b):
    return 1.5 * iterate - 0.5 * jnp.dot(cubic_b[...], iterate_b, preferred_element_type=F32)


def rest_kernel(over_ref, iterate, iterate_b, cubic_b, root_ref):
    width = 2 * TILE
    for s in [slice(n, n + width) for n in range(0, ORDER, width)]:
        new = last_product(iterate[:, s], cubic_b, iterate_b[:, s])
        root_ref[:, s] = (new * over_ref[0:1, 0:1]).astype(BF16)


def right_kernel(over_ref, iterate, iterate_b, cubic_b, *refs):
    slab_refs, right_refs, right = refs[:NZL * NXL], refs[NZL * NXL:NZL * NXL + NZH], refs[-1]
    zh, zl, rows = lax.axis_index("zh"), lax.axis_index("zl"), NY * ROWS
    here = pl.ds(pl.multiple_of(zl * (NZH * TILE), NZH * TILE), NZH * TILE)
    cols = last_product(iterate[:, here], cubic_b, iterate_b[:, here])
    cols = (cols * over_ref[0:1, 0:1]).astype(BF16)
    for turn, ref in enumerate(slab_refs):
        at = (lax.rem(zl + turn // NXL, NZL) * NXL + turn % NXL) * rows
        right[pl.ds(pl.multiple_of(at, rows), rows), :] = jnp.dot(
            ref[...], cols, preferred_element_type=F32
        ).astype(BF16)
    for shift, ref in zip(SHIFTS, right_refs):
        at = lax.rem(zh + shift, NZH) * TILE
        ref[...] = right[:, pl.ds(pl.multiple_of(at, TILE), TILE)]


def left_kernel(root_ref, *refs):
    right_refs, (out_ref, right) = refs[:NZH], refs[NZH:]
    for shift, ref in zip(SHIFTS, right_refs):
        at = lax.rem(lax.axis_index("zh") + NZH - shift, NZH) * ZROWS
        right[pl.ds(pl.multiple_of(at, ZROWS), ZROWS), :] = ref[...]
    out_ref[...] = jnp.dot(root_ref[...], right[...], preferred_element_type=F32).astype(BF16)


def place_kernel(got_ref, out_ref):
    own = block_here()
    for k in range(NBLOCK):
        y = jnp.bitwise_xor(own, flip(k))
        for z in range(NZ):
            at = k * ORDER + z % NZL * (NZH * TILE) + z // NZL * TILE
            out_ref[0, :, at:at + TILE] = got_ref[z * NXL * NY + y]


def place(xl, y, block):
    return (xl * NY + y) * NBLOCK + block


def turned(x, axes, size, shift):
    return lax.ppermute(x, axes, [(n, (n + shift) % size) for n in range(size)])


def local(acts, grads_out, gradient):
    all_tokens = acts.shape[0] * NZ * NXL * NY
    packed = call(
        gram_kernel,
        "gram",
        jax.ShapeDtypeStruct((NZL * NXL * NY, PIECE + REST, TILE), BF16),
        (acts, grads_out),
        specs=[HBM] * 2,
        out_specs=HBM,
        scratch=[
            pltpu.VMEM(acts.shape, BF16),
            pltpu.VMEM(acts.shape, BF16),
            pltpu.VMEM((NZL * NXL * NY, PIECE + REST, TILE), BF16),
            pltpu.SemaphoreType.DMA((2, LOADS)),
            pltpu.SemaphoreType.DMA((2, NZL * NY)),
        ],
        flops=4 * acts.shape[0] * ORDER * ORDER,
        vmem=60 << 20,
    )

    got = lax.all_to_all(packed, ("zl", "xl", "y"), 0, 0, tiled=True)
    part, *turns = call(
        sum_kernel,
        "sum",
        [jax.ShapeDtypeStruct((PIECE + REST, TILE), BF16)]
        + [jax.ShapeDtypeStruct((ROWS, ORDER), BF16)] * NY,
        (got, gradient),
    )
    turns = [turns[0]] + [turned(turns[shift], "y", NY, shift) for shift in range(1, NY)]
    parts = [part] + [turned(part, "zh", NZH, shift) for shift in SHIFTS if shift]
    pieces, done = call(
        functools.partial(damp_kernel, float(all_tokens)),
        "damp",
        [
            jax.ShapeDtypeStruct((NZL * NY, PIECE + REST, TILE), BF16),
            jax.ShapeDtypeStruct((8, TILE), F32),
        ],
        tuple(parts),
        out_specs=[HBM, VMEM],
        scratch=[
            pltpu.VMEM((PIECE + REST, TILE), BF16),
            pltpu.SemaphoreType.DMA((NZL * NY,)),
        ],
    )
    slab = call(
        join_kernel, "join", jax.ShapeDtypeStruct((NY * ROWS, ORDER), BF16), (done, *turns)
    )
    count = NXL * NY * NBLOCK
    cells = [(partner(k, y), k, y) for k in range(NBLOCK) for y in range(NY)]
    slabs = [
        lax.ppermute(
            slab,
            ("zl", "xl", "y", "xh", "c"),
            [
                ((zl + turn) % NZL * count + place(xl, y, i), zl * count + place(1, y, k))
                for zl in range(NZL)
                for i, k, y in cells
            ],
        )
        for turn in range(NZL)
        for xl in range(NXL)
    ]
    packed = lax.all_to_all(pieces, ("zl", "y"), 0, 0, tiled=True)

    square_b = pltpu.VMEM((ORDER, ORDER), BF16)
    right_done = jax.ShapeDtypeStruct((ZROWS, TILE), BF16)
    square = jax.ShapeDtypeStruct((ORDER, ORDER), BF16)
    factors = call(
        root_kernel,
        "root",
        [
            jax.ShapeDtypeStruct((8, TILE), F32),
            jax.ShapeDtypeStruct((ORDER, ORDER), F32),
            square,
            square,
        ],
        (packed,),
        scratch=[square_b, square_b],
        flops=10 * ORDER**3,
    )
    right_done = call(
        right_kernel,
        "right",
        [right_done] * NZH,
        (*factors, *slabs),
        scratch=[pltpu.VMEM((ZROWS, NZH * TILE), BF16)],
        flops=2 * ORDER * (ZROWS + ORDER) * NZH * TILE,
    )
    root = call(rest_kernel, "rest", square, factors, flops=2 * ORDER**3)

    right_done = [
        lax.ppermute(
            right_done[n],
            ("zh", "xl", "y", "xh", "c"),
            [
                (zh * count + place(1, y, k), (zh + shift) % NZH * count + place(0, y, i))
                for zh in range(NZH)
                for i, k, y in cells
            ],
        )
        for n, shift in enumerate(SHIFTS)
    ]
    result = call(
        left_kernel,
        "left",
        jax.ShapeDtypeStruct((ORDER, TILE), BF16),
        (root, *right_done),
        scratch=[pltpu.VMEM((ORDER, TILE), BF16)],
        flops=2 * ORDER * ORDER * TILE,
    )
    result = result.reshape(NZ * NXL * NY, ROWS, TILE)
    returned = lax.all_to_all(result, DP, 0, 0, tiled=True)
    return call(
        place_kernel,
        "place",
        jax.ShapeDtypeStruct((1, ROWS, NBLOCK * ORDER), BF16),
        (returned,),
    )


def solution(mesh):
    split = Mesh(mesh.devices.reshape(SIZES), AXES)
    block = ("xh", "c")
    in_specs = (P(DP, block), P(DP, block), P(block, DP, None))
    out_specs = P(block, DP, None)
    return jax.shard_map(local, mesh=split, in_specs=in_specs, out_specs=out_specs, check_vma=False)
```

```python
import functools

import jax
import jax.numpy as jnp
from jax import lax
from jax.experimental import pallas as pl
from jax.experimental.pallas import tpu as pltpu
from jax.sharding import Mesh, PartitionSpec as P

F32, BF16 = jnp.float32, jnp.bfloat16
SWEEPS = 2
DAMPING = 0.05
TILE = 128
VMEM_BYTES = 28 << 20

AXES = ("zh", "zl", "xl", "y", "xh", "c")
SIZES = (4, 2, 2, 4, 2, 2)
NZH, NZL, NXL, NY, NXH, NC = SIZES
NZ, NBLOCK = NZH * NZL, NXH * NC
DP = ("zh", "zl", "xl", "y")

ORDER = 1024
GRID = ORDER // TILE
PAIRS = [(r, c) for r in range(GRID) for c in range(r, GRID)]
WHERE = {pair: n for n, pair in enumerate(PAIRS)}

HALF = TILE // 2
HALVES = 2 * len(PAIRS) // (NZL * NY)
PIECE = HALVES * HALF
REST = 16
ROWS = 16
TERMS = 3
SHIFTS = (2, 1, 3, 0)
LOADS = 4
ZROWS = NZL * NXL * NY * ROWS


def call(
    kernel, name, out_shape, args, specs=None, out_specs=None, scratch=(), flops=0, vmem=VMEM_BYTES
):
    extra = {} if specs is None else {"in_specs": specs}
    if out_specs is not None:
        extra["out_specs"] = out_specs
    return pl.pallas_call(
        kernel,
        out_shape=out_shape,
        scratch_shapes=list(scratch),
        compiler_params=pltpu.CompilerParams(vmem_limit_bytes=vmem),
        cost_estimate=pl.CostEstimate(flops=flops, bytes_accessed=4 << 20, transcendentals=0),
        name=name,
        **extra,
    )(*args)


HBM = pl.BlockSpec(memory_space=pltpu.HBM)
VMEM = pl.BlockSpec(memory_space=pltpu.VMEM)


def flip(block):
    return block // NC + block % NC * NXH


def partner(block, y):
    return flip(block) ^ y


def flip_scalar(block):
    return lax.div(block, NC) + lax.rem(block, NC) * NXH


def block_here():
    return lax.axis_index("xh") * NC + lax.axis_index("c")


def piece_here():
    return lax.axis_index("zl") * NY + lax.axis_index("y")


def gram_kernel(acts_ref, grads_ref, out_ref, acts, grads, packed, sems, out_sems):
    rows = acts.shape[0] // LOADS
    loads = []
    for which, (far, near) in enumerate(((acts_ref, acts), (grads_ref, grads))):
        for n in range(LOADS):
            part = pl.ds(n * rows, rows)
            loads.append(pltpu.make_async_copy(far.at[part], near.at[part], sems.at[which, n]))
            loads[-1].start()
    width = 2 * TILE
    eye = lax.broadcasted_iota(jnp.int32, (TILE, TILE), 0) == lax.broadcasted_iota(
        jnp.int32, (TILE, TILE), 1
    )
    stores = []
    for which, ref in enumerate((acts, grads)):
        for load in loads[which * LOADS:(which + 1) * LOADS]:
            load.wait()
        rest = {}
        for first in range(0, ORDER, width):
            slab = lax.dot_general(
                ref[:, first:first + width],
                ref[:, first:],
                (((0,), (0,)), ((), ())),
                preferred_element_type=F32,
            )
            for r in range(first // TILE, (first + width) // TILE):
                for c in range(r, GRID):
                    block = slab[
                        r * TILE - first:(r + 1) * TILE - first,
                        c * TILE - first:(c + 1) * TILE - first,
                    ]
                    block_b = block.astype(BF16)
                    for half in range(2):
                        piece, at = divmod(2 * WHERE[(r, c)] + half, HALVES)
                        packed[target_of(which, piece), at * HALF:(at + 1) * HALF] = block_b[
                            half * HALF:(half + 1) * HALF
                        ]
                        if r == c:
                            rest[(piece, at)] = jnp.sum(
                                jnp.where(eye, block - block_b.astype(F32), 0.0), axis=0, keepdims=True
                            )
        for piece in range(NZL * NY):
            lines = [rest.get((piece, at), jnp.zeros((1, TILE), F32)) for at in range(HALVES)]
            put_rest(packed.at[target_of(which, piece)], lines)
        for zl in range(NZL):
            part = pl.ds(target_of(which, zl * NY), NY)
            stores.append(
                pltpu.make_async_copy(packed.at[part], out_ref.at[part], out_sems.at[which, zl])
            )
            stores[-1].start()
    for store in stores:
        store.wait()


def target_of(which, piece):
    return (piece // NY * NXL + which) * NY + piece % NY


def put_rest(ref, lines):
    lines = lines + [jnp.zeros((1, TILE), F32)] * (REST - len(lines))
    ref[PIECE:PIECE + REST] = jnp.concatenate(lines, axis=0).astype(BF16)


def eye_of(piece, at):
    row = lax.broadcasted_iota(jnp.int32, (HALF, TILE), 0)
    return row + lax.rem(piece * HALVES + at, 2) * HALF == lax.broadcasted_iota(
        jnp.int32, (HALF, TILE), 1
    )


def sum_halves(piece, parts):
    def added(rows):
        return sum([part[rows].astype(F32) for part in parts[1:]], parts[0][rows].astype(F32))

    rest = added(slice(PIECE, PIECE + REST))
    halves = []
    for at in range(HALVES):
        total = added(slice(at * HALF, (at + 1) * HALF))
        halves.append(total + jnp.where(eye_of(piece, at), rest[at:at + 1], 0.0))
    return halves


def put_halves(piece, out_ref, halves, more=()):
    lines = []
    for at, half in enumerate(halves):
        half_b = half.astype(BF16)
        lines.append(
            jnp.sum(jnp.where(eye_of(piece, at), half - half_b.astype(F32), 0.0), axis=0, keepdims=True)
        )
        out_ref[at * HALF:(at + 1) * HALF] = half_b
    put_rest(out_ref, lines + list(more))


def sum_kernel(got_ref, gradient_ref, out_ref, *turn_refs):
    y, own = lax.axis_index("y"), block_here()
    for shift, ref in enumerate(turn_refs):
        block = flip_scalar(jnp.bitwise_xor(own, lax.rem(y + shift, NY)))
        start = pl.multiple_of(block * ORDER, ORDER)
        ref[...] = gradient_ref[0, :, pl.ds(start, ORDER)].astype(BF16)
    piece = piece_here()
    put_halves(piece, out_ref, sum_halves(piece, [got_ref.at[n] for n in range(got_ref.shape[0])]))


def damp_kernel(all_tokens, *refs):
    parts, turn_refs = refs[:NZH], refs[NZH:NZH + NY]
    out_ref, slab_ref, damped, sems = refs[NZH + NY:]
    piece = piece_here()
    halves = []
    squares = jnp.zeros((HALF, TILE), F32)
    for at, half in enumerate(sum_halves(piece, parts)):
        block = lax.div(piece * HALVES + at, 2)
        on_diag = functools.reduce(jnp.logical_or, [block == WHERE[(r, r)] for r in range(GRID)])
        damping = jnp.where(on_diag, DAMPING, 0.0)
        half = half / all_tokens + jnp.where(eye_of(piece, at), damping, 0.0)
        squares = squares + jnp.where(on_diag, 1.0, 2.0) * half * half
        halves.append(half)
    left = jnp.sum(jnp.sum(squares, axis=0, keepdims=True), axis=1, keepdims=True)
    left = jnp.broadcast_to(left, (1, TILE))
    terms = []
    for _ in range(TERMS):
        terms.append(left.astype(BF16).astype(F32))
        left = left - terms[-1]
    put_halves(piece, damped, halves, terms)
    stores = [
        pltpu.make_async_copy(damped, out_ref.at[n], sems.at[n]) for n in range(out_ref.shape[0])
    ]
    for store in stores:
        store.start()
    for turn, ref in enumerate(turn_refs):
        at = lax.rem(lax.axis_index("y") + NY - turn, NY) * ROWS
        slab_ref[pl.ds(pl.multiple_of(at, ROWS), ROWS), :] = ref[...]
    for store in stores:
        store.wait()


def root_kernel(packed_ref, over_ref, iterate, iterate_b, cubic_b, scaled, square_b):
    terms = sum([packed_ref[n, PIECE:].astype(F32) for n in range(NZL * NY)])[HALVES:HALVES + TERMS]
    frob = jnp.sqrt(jnp.sum(terms, axis=0, keepdims=True)[:, 0:1])
    over_frob = 1.0 / frob
    over_ref[...] = jnp.broadcast_to(1.0 / jnp.sqrt(frob), over_ref.shape)
    for r, c in PAIRS:
        parts = []
        for half in range(2):
            piece, at = divmod(2 * WHERE[(r, c)] + half, HALVES)
            part = packed_ref[piece, at * HALF:(at + 1) * HALF].astype(F32)
            if r == c:
                rest = packed_ref[piece, PIECE:].astype(F32)[at:at + 1]
                part = part + jnp.where(eye_of(piece, at), rest, 0.0)
            parts.append(part)
        block = (jnp.concatenate(parts, axis=0) * over_frob).astype(BF16)
        scaled[r * TILE:(r + 1) * TILE, c * TILE:(c + 1) * TILE] = block
        if r != c:
            scaled[c * TILE:(c + 1) * TILE, r * TILE:(r + 1) * TILE] = block.T
    width = 2 * TILE
    tiles = [slice(n, n + width) for n in range(0, ORDER, width)]
    for s in tiles:
        row = lax.broadcasted_iota(jnp.int32, (ORDER, width), 0)
        col = lax.broadcasted_iota(jnp.int32, (ORDER, width), 1) + s.start
        first = 1.5 * (row == col).astype(F32) - 0.5 * scaled[:, s].astype(F32)
        iterate[:, s] = first
        iterate_b[:, s] = first.astype(BF16)
    for sweep in range(SWEEPS):
        for left, other, out in ((iterate_b, iterate_b, square_b), (square_b, scaled, cubic_b)):
            for s in tiles:
                upper = jnp.dot(
                    left[:s.stop], other[:, s], preferred_element_type=F32
                ).astype(BF16)
                out[:s.stop, s] = upper
                for t in tiles[:s.start // width]:
                    out[s, t] = upper[t].T
        if sweep < SWEEPS - 1:
            for s in tiles:
                iterate[:, s] = last_product(iterate[:, s], cubic_b, iterate_b[:, s])
            for s in tiles:
                iterate_b[:, s] = iterate[:, s].astype(BF16)


def last_product(iterate, cubic_b, iterate_b):
    return 1.5 * iterate - 0.5 * jnp.dot(cubic_b[...], iterate_b, preferred_element_type=F32)


def rest_kernel(over_ref, iterate, iterate_b, cubic_b, root_ref):
    width = 2 * TILE
    for s in [slice(n, n + width) for n in range(0, ORDER, width)]:
        new = last_product(iterate[:, s], cubic_b, iterate_b[:, s])
        root_ref[:, s] = (new * over_ref[0:1, 0:1]).astype(BF16)


def right_kernel(over_ref, iterate, iterate_b, cubic_b, *refs):
    slab_refs, right_refs, right = refs[:NZL * NXL], refs[NZL * NXL:NZL * NXL + NZH], refs[-1]
    zh, zl, rows = lax.axis_index("zh"), lax.axis_index("zl"), NY * ROWS
    here = pl.ds(pl.multiple_of(zl * (NZH * TILE), NZH * TILE), NZH * TILE)
    cols = last_product(iterate[:, here], cubic_b, iterate_b[:, here])
    cols = (cols * over_ref[0:1, 0:1]).astype(BF16)
    for turn, ref in enumerate(slab_refs):
        at = (lax.rem(zl + turn // NXL, NZL) * NXL + turn % NXL) * rows
        right[pl.ds(pl.multiple_of(at, rows), rows), :] = jnp.dot(
            ref[...], cols, preferred_element_type=F32
        ).astype(BF16)
    for shift, ref in zip(SHIFTS, right_refs):
        at = lax.rem(zh + shift, NZH) * TILE
        ref[...] = right[:, pl.ds(pl.multiple_of(at, TILE), TILE)]


def left_kernel(root_ref, *refs):
    right_refs, (out_ref, right) = refs[:NZH], refs[NZH:]
    for shift, ref in zip(SHIFTS, right_refs):
        at = lax.rem(lax.axis_index("zh") + NZH - shift, NZH) * ZROWS
        right[pl.ds(pl.multiple_of(at, ZROWS), ZROWS), :] = ref[...]
    out_ref[...] = jnp.dot(root_ref[...], right[...], preferred_element_type=F32).astype(BF16)


def place_kernel(got_ref, out_ref):
    own = block_here()
    for k in range(NBLOCK):
        y = jnp.bitwise_xor(own, flip(k))
        for z in range(NZ):
            at = k * ORDER + z % NZL * (NZH * TILE) + z // NZL * TILE
            out_ref[0, :, at:at + TILE] = got_ref[z * NXL * NY + y]


def place(xl, y, block):
    return (xl * NY + y) * NBLOCK + block


def turned(x, axes, size, shift):
    return lax.ppermute(x, axes, [(n, (n + shift) % size) for n in range(size)])


def local(acts, grads_out, gradient):
    all_tokens = acts.shape[0] * NZ * NXL * NY
    packed = call(
        gram_kernel,
        "gram",
        jax.ShapeDtypeStruct((NZL * NXL * NY, PIECE + REST, TILE), BF16),
        (acts, grads_out),
        specs=[HBM] * 2,
        out_specs=HBM,
        scratch=[
            pltpu.VMEM(acts.shape, BF16),
            pltpu.VMEM(acts.shape, BF16),
            pltpu.VMEM((NZL * NXL * NY, PIECE + REST, TILE), BF16),
            pltpu.SemaphoreType.DMA((2, LOADS)),
            pltpu.SemaphoreType.DMA((2, NZL)),
        ],
        flops=4 * acts.shape[0] * ORDER * ORDER,
        vmem=60 << 20,
    )

    got = lax.all_to_all(packed, ("zl", "xl", "y"), 0, 0, tiled=True)
    part, *turns = call(
        sum_kernel,
        "sum",
        [jax.ShapeDtypeStruct((PIECE + REST, TILE), BF16)]
        + [jax.ShapeDtypeStruct((ROWS, ORDER), BF16)] * NY,
        (got, gradient),
    )
    turns = [turns[0]] + [turned(turns[shift], "y", NY, shift) for shift in range(1, NY)]
    parts = [part] + [turned(part, "zh", NZH, shift) for shift in SHIFTS[2::-1]]
    pieces, slab = call(
        functools.partial(damp_kernel, float(all_tokens)),
        "damp",
        [
            jax.ShapeDtypeStruct((NZL * NY, PIECE + REST, TILE), BF16),
            jax.ShapeDtypeStruct((NY * ROWS, ORDER), BF16),
        ],
        (*parts, *turns),
        out_specs=[HBM, VMEM],
        scratch=[
            pltpu.VMEM((PIECE + REST, TILE), BF16),
            pltpu.SemaphoreType.DMA((NZL * NY,)),
        ],
    )
    count = NXL * NY * NBLOCK
    cells = [(partner(k, y), k, y) for k in range(NBLOCK) for y in range(NY)]
    slabs = [
        lax.ppermute(
            slab,
            ("zl", "xl", "y", "xh", "c"),
            [
                ((zl + turn) % NZL * count + place(xl, y, i), zl * count + place(1, y, k))
                for zl in range(NZL)
                for i, k, y in cells
            ],
        )
        for turn in range(NZL)
        for xl in range(NXL)
    ]
    packed = lax.all_to_all(pieces, ("zl", "y"), 0, 0, tiled=True)

    square_b = pltpu.VMEM((ORDER, ORDER), BF16)
    right_done = jax.ShapeDtypeStruct((ZROWS, TILE), BF16)
    square = jax.ShapeDtypeStruct((ORDER, ORDER), BF16)
    factors = call(
        root_kernel,
        "root",
        [
            jax.ShapeDtypeStruct((8, TILE), F32),
            jax.ShapeDtypeStruct((ORDER, ORDER), F32),
            square,
            square,
        ],
        (packed,),
        scratch=[square_b, square_b],
        flops=10 * ORDER**3,
    )
    right_done = call(
        right_kernel,
        "right",
        [right_done] * NZH,
        (*factors, *slabs),
        scratch=[pltpu.VMEM((ZROWS, NZH * TILE), BF16)],
        flops=2 * ORDER * (ZROWS + ORDER) * NZH * TILE,
    )
    root = call(rest_kernel, "rest", square, factors, flops=2 * ORDER**3)

    right_done = [
        lax.ppermute(
            right_done[n],
            ("zh", "xl", "y", "xh", "c"),
            [
                (zh * count + source, (zh + shift) % NZH * count + target)
                for zh in range(NZH)
                for i, k, y in cells
                for source, target in (
                    (place(1, y, k), place(0, y, i)),
                    (place(0, y, i), place(1, y, k)),
                )
            ],
        )
        for n, shift in enumerate(SHIFTS)
    ]
    result = call(
        left_kernel,
        "left",
        jax.ShapeDtypeStruct((ORDER, TILE), BF16),
        (root, *right_done),
        scratch=[pltpu.VMEM((ORDER, TILE), BF16)],
        flops=2 * ORDER * ORDER * TILE,
    )
    result = result.reshape(NZ * NXL * NY, ROWS, TILE)
    returned = lax.all_to_all(result, DP, 0, 0, tiled=True)
    return call(
        place_kernel,
        "place",
        jax.ShapeDtypeStruct((1, ROWS, NBLOCK * ORDER), BF16),
        (returned,),
    )


def solution(mesh):
    split = Mesh(mesh.devices.reshape(SIZES), AXES)
    block = ("xh", "c")
    in_specs = (P(DP, block), P(DP, block), P(block, DP, None))
    out_specs = P(block, DP, None)
    return jax.shard_map(local, mesh=split, in_specs=in_specs, out_specs=out_specs, check_vma=False)
```
